32 devices in a mesh: freq: 8 (over z, y), sta: 4 (over x, core).
Axes of the slice: x: 2, y: 2, z: 4, core: 2. Of those that a mesh axis runs over, the one named last changes fastest.
Arguments:
- spectra: float32 [2, 128, 64, 8192], P(None, 'freq', None, 'sta'), may hold values from -24 to 24
- current: float32 [64, 2, 128, 512], P('freq', None, None, 'sta'), may hold values from -600 to 600, as said below
- previous: float32 [64, 2, 128, 512], P('freq', None, None, 'sta'), may hold values from -600 to 600, as said below
- table: int32 [64, 512], replicated, may hold values from 0 to 16383
- station_block: int32 [8192], P('sta'), may hold values from 0 to 63
- offsets: float32 [2, 8192], P(None, 'sta'), may hold values from -4 to 4
- slowness: float32 [2, 512], replicated, may hold values from -3 to 3
- weights: float32 [512], P('sta'), may hold values from 400 to 5000
- momentum: float32 [1], replicated, may hold values from 2 to 10
Outputs:
- estimate: float32 [64, 2, 128, 512], P('freq', None, None, 'sta')
- extrapolated: float32 [64, 2, 128, 512], P('freq', None, None, 'sta')
The draws below stay inside these ranges and needn't reach their ends.
Inputs may be any that keep to these rules, and one draw needn't show every extreme that they name: `current`: real values. `previous`: real values.
All inputs are finite; a program needn't handle non-finite values.
Results may differ from the reference program's by a relative error of at most 0.00105.
The reference program's roundings to bfloat16 on the way count: a program that leaves them out, or rounds other values in their place, can miss the bound.
Values may be sent and summed in bfloat16 or wider, within the bound.
A program may use at most 192 MiB of HBM per device.

```python
import math
import jax
import jax.numpy as jnp
from jax import lax

F = 64
CELLS = 512
W = 128
NB = 64
TMAX = 16384
STATIONS = 8192


def iterate_draw(key, stream_tag):
    shared = jax.random.fold_in(key, 101)
    bin_key, cell_key = jax.random.split(shared, 2)
    noise_key = jax.random.fold_in(key, stream_tag)
    bin_pos = jnp.arange(F, dtype=jnp.float32) / (F - 1)
    bin_scale = 10.0 ** bin_pos * jnp.exp(jax.random.uniform(bin_key, (F,), jnp.float32, -0.35, 0.35))
    cell_scale = 10.0 ** jax.random.uniform(cell_key, (CELLS,), jnp.float32)
    fluctuation = jnp.clip(jax.random.normal(noise_key, (F, 2, W, CELLS), jnp.float32), -4.0, 4.0)
    return fluctuation * bin_scale[:, None, None, None] * cell_scale[None, None, None, :]


def draw_current(key, part):
    return iterate_draw(key, 7)


def draw_previous(key, part):
    return iterate_draw(key, 13)


def plant(drawn, rng, low, top_value):
    longest = drawn.shape.index(max(drawn.shape))
    spots = []
    for shift in (0, 1):
        where = [jax.random.randint(jax.random.fold_in(rng, axis), (), 0, length) for axis, length in enumerate(drawn.shape)]
        where[longest] = (where[longest] + shift) % drawn.shape[longest]
        spots.append(tuple(where))
    return drawn.at[spots[0]].set(low).at[spots[1]].set(top_value)


def shard_levels(own_key, dims, cuts, smallest, top_value):
    level = 1.0
    for dim, blocks in cuts:
        heights = jax.random.uniform(jax.random.fold_in(jax.random.fold_in(own_key, 6), dim), (blocks,), jnp.float32, smallest / len(cuts), top_value / len(cuts))
        level = level * jnp.repeat(jnp.exp(heights), dims[dim] // blocks).reshape((-1,) + (1,) * (len(dims) - 1 - dim))
    return level


def noise(stream_key, dims, spread, reach, shards=(), kind=jnp.bfloat16):
    drawn = spread * jax.random.normal(stream_key, dims, jnp.float32)
    if shards:
        drawn = drawn * shard_levels(stream_key, dims, shards, -0.22, 0.18)
    return jnp.clip(drawn, -reach, reach).astype(kind)


def setup_inputs(seed: int = 0) -> dict:
    splits = jax.random.split(jax.random.key(seed), 10)
    spectra = noise(splits[0], (2, W, F, STATIONS), 4.0, 24.0, ((1, 8), (3, 4)), jnp.float32)
    current = draw_current(jax.random.fold_in(splits[9], 71), 0)
    previous = draw_previous(jax.random.fold_in(splits[9], 71), 0)
    table = plant(jax.random.randint(splits[3], (NB, CELLS), 0, TMAX), jax.random.fold_in(splits[3], 1), 0, TMAX - 1).astype(jnp.int32)
    station_block = plant(jax.random.randint(splits[4], (STATIONS,), 0, NB), jax.random.fold_in(splits[4], 1), 0, NB - 1).astype(jnp.int32)
    offsets = noise(splits[5], (2, STATIONS), 1.0, 4.0, ((1, 4),), jnp.float32)
    slowness = jnp.clip(jax.random.uniform(splits[6], (2, CELLS), jnp.float32, -3.0, 3.0), -3.0, 3.0)
    weights = jnp.clip(jnp.exp(math.log(5000.0) - 2.5257286 * jax.random.uniform(splits[7], (CELLS,), jnp.float32) ** shard_levels(splits[7], (CELLS,), ((0, 4),), -0.2, 0.2)), 400.0, 5000.0)
    momentum = jnp.clip(jax.random.uniform(splits[8], (1,), jnp.float32, 2.0, 10.0), 2.0, 10.0)
    return {"spectra": spectra, "current": current, "previous": previous, "table": table, "station_block": station_block, "offsets": offsets, "slowness": slowness, "weights": weights, "momentum": momentum}


def cell_block(cell_count):
    block_len = cell_count
    while block_len > 512 and block_len % 2 == 0:
        block_len = block_len // 2
    return block_len

def phases(number, delay_rows, off_rows, slow_cols, period):
    wrapped = number * delay_rows % period
    geometry = off_rows[0][:, None] * slow_cols[0][None, :] + off_rows[1][:, None] * slow_cols[1][None, :]
    phase_angle = (wrapped.astype(jnp.float32) + number.astype(jnp.float32) * geometry) * (2.0 * math.pi / period)
    return (jnp.cos(phase_angle).astype(jnp.bfloat16), jnp.sin(phase_angle).astype(jnp.bfloat16))

def forward_terms(cos_part, sin_part, iterate):
    window_count = iterate.shape[1]
    stacked = iterate.reshape(2 * window_count, iterate.shape[2])
    contract = (((1,), (1,)), ((), ()))
    with_cos = lax.dot_general(stacked, cos_part, contract, preferred_element_type=jnp.float32)
    with_sin = lax.dot_general(stacked, sin_part, contract, preferred_element_type=jnp.float32)
    real_part = with_cos[:window_count] + with_sin[window_count:]
    imag_part = with_cos[window_count:] - with_sin[:window_count]
    return jnp.stack([real_part, imag_part])

def adjoint_terms(cos_part, sin_part, residual):
    window_count = residual.shape[1]
    stacked = residual.reshape(2 * window_count, residual.shape[2])
    with_cos = jnp.dot(stacked, cos_part, preferred_element_type=jnp.float32)
    with_sin = jnp.dot(stacked, sin_part, preferred_element_type=jnp.float32)
    real_part = with_cos[:window_count] - with_sin[window_count:]
    imag_part = with_cos[window_count:] + with_sin[:window_count]
    return jnp.stack([real_part, imag_part])

def reference(spectra, current, previous, table, station_block, offsets, slowness, weights, momentum):
    period = 4 * F
    normalizer = 1.0 / math.sqrt(CELLS)
    block_len = cell_block(CELLS)
    relaid = jnp.transpose(spectra, (2, 0, 1, 3))

    def one_bin(bin_inputs):
        number, iterate, observed = bin_inputs
        iterate_b = iterate.astype(jnp.bfloat16)
        running = jnp.zeros((2, W, STATIONS), jnp.float32)
        for first_cell in range(0, CELLS, block_len):
            delay_rows = jnp.take(table[:, first_cell:first_cell + block_len], station_block, axis=0)
            cos_part, sin_part = phases(number, delay_rows, offsets, slowness[:, first_cell:first_cell + block_len], period)
            running = running + forward_terms(cos_part, sin_part, iterate_b[:, :, first_cell:first_cell + block_len])
        residual = (running * normalizer - observed).astype(jnp.bfloat16)
        pieces = []
        for first_cell in range(0, CELLS, block_len):
            delay_rows = jnp.take(table[:, first_cell:first_cell + block_len], station_block, axis=0)
            cos_part, sin_part = phases(number, delay_rows, offsets, slowness[:, first_cell:first_cell + block_len], period)
            pieces.append(adjoint_terms(cos_part, sin_part, residual) * normalizer)
        return jnp.concatenate(pieces, axis=2)
    numbers = jnp.arange(1, F + 1, dtype=jnp.int32)
    gradient = lax.map(one_bin, (numbers, current, relaid))
    step_size = CELLS / (math.sqrt(STATIONS) + math.sqrt(CELLS)) ** 2
    stepped = current - step_size * gradient
    group_norm = jnp.sqrt(lax.optimization_barrier(jnp.sum(stepped * stepped, axis=(0, 1))) + 1e-06)
    estimate = stepped * jnp.maximum(0.0, 1.0 - step_size * weights[None, :] / group_norm)
    momentum_now = momentum[0]
    momentum_next = (1.0 + jnp.sqrt(1.0 + 4.0 * momentum_now * momentum_now)) / 2.0
    extrapolated = estimate + (momentum_now - 1.0) / momentum_next * (estimate - previous)
    return (estimate, extrapolated)
```

```python
import functools
import math

import jax
import jax.numpy as jnp
from jax import lax
from jax.experimental import pallas as pl
from jax.experimental.pallas import tpu as pltpu
from jax.sharding import PartitionSpec as P

F = 64
CELLS = 512


def cell_block(cell_count):
    block_len = cell_count
    while block_len > 512 and block_len % 2 == 0:
        block_len = block_len // 2
    return block_len


def phases(number, delay_rows, off_rows, slow_cols, period):
    wrapped = number * delay_rows % period
    geometry = (
        off_rows[0][:, None] * slow_cols[0][None, :] + off_rows[1][:, None] * slow_cols[1][None, :]
    )
    phase_angle = (wrapped.astype(jnp.float32) + number.astype(jnp.float32) * geometry) * (
        2.0 * math.pi / period
    )
    return (jnp.cos(phase_angle).astype(jnp.bfloat16), jnp.sin(phase_angle).astype(jnp.bfloat16))


def forward_terms(cos_part, sin_part, iterate):
    window_count = iterate.shape[1]
    stacked = iterate.reshape(2 * window_count, iterate.shape[2])
    contract = (((1,), (1,)), ((), ()))
    with_cos = lax.dot_general(stacked, cos_part, contract, preferred_element_type=jnp.float32)
    with_sin = lax.dot_general(stacked, sin_part, contract, preferred_element_type=jnp.float32)
    real_part = with_cos[:window_count] + with_sin[window_count:]
    imag_part = with_cos[window_count:] - with_sin[:window_count]
    return jnp.stack([real_part, imag_part])


def adjoint_terms(cos_part, sin_part, residual):
    window_count = residual.shape[1]
    stacked = residual.reshape(2 * window_count, residual.shape[2])
    with_cos = jnp.dot(stacked, cos_part, preferred_element_type=jnp.float32)
    with_sin = jnp.dot(stacked, sin_part, preferred_element_type=jnp.float32)
    real_part = with_cos[:window_count] - with_sin[window_count:]
    imag_part = with_cos[window_count:] + with_sin[:window_count]
    return jnp.stack([real_part, imag_part])


def local(spectra, current, previous, table, station_block, offsets, slowness, weights, momentum):
    period = 4 * F
    normalizer = 1.0 / math.sqrt(CELLS)
    bin_count = current.shape[0]
    cell_share = current.shape[3]
    stations_here = station_block.shape[0]
    station_total = stations_here * lax.axis_size("sta")
    first_bin = lax.axis_index("freq") * bin_count
    relaid = lax.all_to_all(
        spectra.astype(jnp.bfloat16), "freq", split_axis=2, concat_axis=1, tiled=True
    ).astype(spectra.dtype)
    iterate_b = current.astype(jnp.bfloat16)
    segment = lax.all_gather(iterate_b, "sta", axis=3, tiled=True)
    cell_count = segment.shape[3]
    block_len = cell_block(cell_count)
    delay_rows = jnp.take(table, station_block, axis=0)
    bin_terms = []
    cos_blocks = []
    sin_blocks = []
    for add_bin_index in range(bin_count):
        cos_part, sin_part = phases(
            first_bin + add_bin_index + 1, delay_rows, offsets, slowness, period
        )
        cos_blocks.append(cos_part)
        sin_blocks.append(sin_part)
        bin_terms.append(
            forward_terms(cos_part, sin_part, segment[add_bin_index, :, :, 0:block_len])
        )
    running = jnp.stack(bin_terms)
    cos_all = jnp.stack(cos_blocks)
    sin_all = jnp.stack(sin_blocks)
    predicted, cos_all, sin_all = (running, cos_all, sin_all)
    bin_sums = []
    for bin_index in range(bin_count):
        residual = (predicted[bin_index] * normalizer - relaid[:, :, bin_index, :]).astype(
            jnp.bfloat16
        )
        bin_sums.append(
            adjoint_terms(cos_all[bin_index], sin_all[bin_index], residual) * normalizer
        )
    partial_sums = jnp.stack(bin_sums)
    summed = lax.psum(partial_sums, "sta")
    gradient = lax.dynamic_slice_in_dim(summed, lax.axis_index("sta") * cell_share, cell_share, 3)
    step_size = CELLS / (math.sqrt(station_total) + math.sqrt(CELLS)) ** 2
    stepped = current - step_size * gradient
    threshold = step_size * weights
    squares = jnp.sum(stepped * stepped, axis=(0, 1))
    group_norm = jnp.sqrt(lax.psum(squares, "freq") + 1e-06)
    estimate = stepped * jnp.maximum(0.0, 1.0 - threshold[None, :] / group_norm)
    momentum_now = momentum[0]
    momentum_next = (1.0 + jnp.sqrt(1.0 + 4.0 * momentum_now * momentum_now)) / 2.0
    extrapolated = estimate + (momentum_now - 1.0) / momentum_next * (estimate - previous)
    return (estimate, extrapolated)


SIN_TERMS = (3.1415926535362892, -5.167712764624382, 2.5501633189428987, -0.5992521977810126, 0.08205040162239277, -0.007028386120383206)
COS_TERMS = (0.9999999997799041, -4.934802137078749, 4.058709159554242, -1.335212003029471, 0.23493731372678894, -0.024396324214549327)
MESH = pl.DeviceIdType.MESH
TILE = 512
ROWS = 32
COLS = 256
UNITS = 16
SBUF = 4
STAGE = 2


def horner(terms, u):
    total = jnp.full_like(u, terms[-1])
    for term in terms[-2::-1]:
        total = total * u + term
    return total


def turns_cos_sin(turns):
    part = turns - jnp.round(turns)
    square = part * part
    half_sin = part * horner(SIN_TERMS, square)
    half_cos = horner(COS_TERMS, square)
    doubled = half_sin + half_sin
    return 1.0 - doubled * half_sin, doubled * half_cos


def times(a, b):
    return a[0] * b[0] - a[1] * b[1], a[1] * b[0] + a[0] * b[1]


def twice(a):
    doubled = a[1] + a[1]
    return 1.0 - doubled * a[1], doubled * a[0]


def iteration_kernel(
    period, normalizer, step_size,
    spectra, current, table, blocks, offsets, slowness, weights,
    stepped_out, shrink_out,
    cs_a, cs_b, prev_cos, prev_sin, now_cos, now_sin, unit_cos, unit_sin, chain,
    tab_t, slow_t, delay,
    current_b, x_all, spec_rx, sbuf, stage, own, home, gbuf, rx1, rx2, tx2, keep2, tx3, sums, shrinks,
    x_send, x_recv, y_send, y_recv, s_send, s_recv, l_stage, l_own,
    g1_send, g1_recv, g2_send, g2_recv, g3_send, g3_recv, n_send, n_recv, m_send, m_recv,
):
    me = lax.axis_index("freq")
    sta = lax.axis_index("sta")
    z, y = me // 2, me % 2
    zl, zp = z % 2, z // 2
    x, core = sta // 2, sta % 2
    tiles = cs_a.shape[1]

    def pick(ph, first, second):
        return jnp.where(ph == 0, first, second)

    def block_of(ph, fd, m):
        return pick(ph, fd // 2 * 2 + m, (fd // 4 * 2 + m) * 2 + fd % 2)

    def residue_of(ph, fd):
        return pick(ph, 2 * (fd % 2), 1 + 2 * (fd // 2 % 2))

    def member(ph):
        return pick(ph, y, zl)

    def partner(ph):
        return pick(ph, me ^ 1, me ^ 2)

    def stage_copy(ph, unit):
        slot = lax.rem(unit, STAGE)
        line = 4 * unit + residue_of(ph, partner(ph))
        return pltpu.make_async_copy(spectra.at[:, :, line, :], stage.at[ph, slot], l_stage.at[ph, slot])

    def own_copy(q, par, e):
        ph = q // 8
        line = 4 * (2 * (q % 8) + e) + residue_of(ph, me)
        return pltpu.make_async_copy(spectra.at[:, :, line, :], own.at[par, e], l_own.at[par, e])

    for first in range(STAGE):
        for ph in range(2):
            stage_copy(ph, first).start()
    for e in range(2):
        own_copy(0, 0, e).start()

    barrier = pltpu.get_barrier_semaphore()
    for d in range(1, 8):
        pl.semaphore_signal(barrier, inc=1, device_id=(me ^ d, sta), device_id_type=MESH)
    for d in range(1, 4):
        pl.semaphore_signal(barrier, inc=1, device_id=(me, sta ^ d), device_id_type=MESH)
    for j in range(8):
        current_b[j // 4, j % 4] = current[j].astype(jnp.bfloat16)
    pl.semaphore_wait(barrier, 10)

    def x_remote(ph, fd, m, source, origin):
        return pltpu.make_async_remote_copy(
            current_b.at[:, residue_of(ph, fd), :, pl.ds(pl.multiple_of(16 * block_of(ph, fd, m), 16), 16), :],
            x_all.at[sta, pl.ds(8 * 2 * ph + 2 * origin, 2), :, pl.ds(16 * m, 16), :],
            x_send.at[ph, m, source], x_recv.at[ph, m, origin],
            device_id=(fd, sta), device_id_type=MESH,
        )

    def x_local(ph, m):
        return pltpu.make_async_copy(
            current_b.at[:, residue_of(ph, me), :, pl.ds(pl.multiple_of(16 * block_of(ph, me, m), 16), 16), :],
            x_all.at[sta, pl.ds(8 * 2 * ph + 2 * me, 2), :, pl.ds(16 * m, 16), :],
            x_recv.at[ph, m, me],
        )

    for ph in range(2):
        for m in range(2):
            x_local(ph, m).start()
        for d in range(1, 8):
            for m in range(2):
                x_remote(ph, me ^ d, m, d, me).start()

    def forward(ph, origin):
        for m in range(2):
            @pl.when(origin == me)
            def _():
                x_local(ph, m).wait()

            @pl.when(origin != me)
            def _():
                x_remote(ph, me, m, 1, origin).wait_recv()
        for d in range(1, 4):
            y_remote(ph, origin, d).start()

    def y_remote(ph, origin, d):
        rows = pl.ds(8 * 2 * ph + 2 * origin, 2)
        return pltpu.make_async_remote_copy(
            x_all.at[sta, rows], x_all.at[sta, rows],
            y_send.at[ph, origin, d], y_recv.at[ph, origin, d],
            device_id=(me, sta ^ d), device_id_type=MESH,
        )

    def s_remote(ph, unit):
        slot = lax.rem(unit, SBUF)
        return pltpu.make_async_remote_copy(
            sbuf.at[ph, slot], spec_rx.at[ph, unit], s_send.at[ph, slot], s_recv.at[ph, unit],
            device_id=(partner(ph), sta), device_id_type=MESH,
        )

    def send_unit(unit):
        for ph in range(2):
            stage_copy(ph, unit).wait()

            @pl.when(unit >= SBUF)
            def _():
                s_remote(ph, unit - SBUF).wait_send()

            sbuf[ph, lax.rem(unit, SBUF)] = stage[ph, lax.rem(unit, STAGE)].astype(jnp.bfloat16)
            s_remote(ph, unit).start()

            @pl.when(unit + STAGE < UNITS)
            def _():
                stage_copy(ph, unit + STAGE).start()

    tab_t[...] = jnp.transpose(jnp.bitwise_and(table[...], period - 1).astype(jnp.float32)).astype(jnp.bfloat16)
    slow_t[...] = jnp.transpose(slowness[...])
    cells = delay.shape[0]
    scale = 1.0 / period

    def strips():
        for r in range(0, cells, ROWS):
            for c in range(0, TILE, COLS):
                yield slice(r, r + ROWS), slice(c, c + COLS), slice(TILE + c, TILE + c + COLS)

    def start_chain(ph, unit, turn, cs, t, at):
        row, col, col_s = at
        second = twice(unit)
        if ph == 0:
            third = times(unit, second)
            a = jnp.where(y == 0, third[0], unit[0]), -jnp.where(y == 0, third[1], unit[1])
            b = jnp.where(y == 0, unit[0], third[0]), jnp.where(y == 0, unit[1], third[1])
        else:
            fourth = twice(second)
            a = jnp.where(zl == 0, second[0], 1.0), jnp.where(zl == 0, -second[1], 0.0)
            b = jnp.where(zl == 0, second[0], fourth[0]), jnp.where(zl == 0, second[1], fourth[1])
        store_pair(a, b, turn, cs, t, at, first=True)

    def store_pair(a, b, turn, cs, t, at, first):
        row, col, col_s = at
        one = b if first else (turn * b[0] - a[0], turn * b[1] - a[1])
        old = a if first else b
        two = turn * one[0] - old[0], turn * one[1] - old[1]
        prev_cos[t, row, col], prev_sin[t, row, col] = one
        now_cos[t, row, col], now_sin[t, row, col] = two
        for e, value in enumerate((one, two)):
            cs[e, t, row, col] = value[0].astype(jnp.bfloat16)
            cs[e, t, row, col_s] = value[1].astype(jnp.bfloat16)

    def angles(t, _):
        lanes = pl.ds(pl.multiple_of(t * TILE, TILE), TILE)
        picks = lax.broadcasted_iota(jnp.int32, (tab_t.shape[1], TILE), 0)
        picks = jnp.where(picks == blocks[:, lanes], 1.0, 0.0).astype(jnp.bfloat16)
        delay[...] = jnp.dot(tab_t[...], picks, preferred_element_type=jnp.float32)

        def strip(index, _):
            r = pl.multiple_of(index * ROWS, ROWS)
            row = pl.ds(r, ROWS)
            slow = slow_t[row, :]
            for c in range(0, TILE, COLS):
                col, col_s = slice(c, c + COLS), slice(TILE + c, TILE + c + COLS)
                here = pl.ds(pl.multiple_of(t * TILE + c, COLS), COLS)
                geometry = offsets[0:1, here] * slow[:, 0:1] + offsets[1:2, here] * slow[:, 1:2]
                turns = delay[row, col] * scale
                unit = turns_cos_sin((delay[row, col] + geometry) * scale)
                turns = 4.0 * turns
                fourth, _ = turns_cos_sin((turns - jnp.round(turns)) + geometry * (4.0 * scale))
                turn = fourth + fourth
                unit_cos[t, row, col], unit_sin[t, row, col] = unit
                chain[t, row, col] = turn
                start_chain(0, unit, turn, cs_a, t, (row, col, col_s))
            return 0

        lax.fori_loop(0, cells // ROWS, strip, 0)
        send_unit(t)
        return 0

    lax.fori_loop(0, tiles, angles, 0)

    def again(t, _):
        def strip(index, _):
            row = pl.ds(pl.multiple_of(index * ROWS, ROWS), ROWS)
            for c in range(0, TILE, COLS):
                col, col_s = slice(c, c + COLS), slice(TILE + c, TILE + c + COLS)
                unit = unit_cos[t, row, col], unit_sin[t, row, col]
                start_chain(1, unit, chain[t, row, col], cs_a, t, (row, col, col_s))
            return 0

        lax.fori_loop(0, cells // ROWS, strip, 0)
        return 0

    def forward_all(origin, _):
        forward(0, origin)
        return 0

    lax.fori_loop(0, 8, forward_all, 0)

    across = (((1,), (1,)), ((), ()))

    def g1_remote(q, par, k):
        share = 1 - core + 2 * k
        return pltpu.make_async_remote_copy(
            gbuf.at[par, share], rx1.at[lax.rem(q, 4), k], g1_send.at[par, k], g1_recv.at[lax.rem(q, 4), k],
            device_id=(me, sta ^ 1), device_id_type=MESH,
        )

    def g2_remote(q, par):
        return pltpu.make_async_remote_copy(
            tx2.at[par], rx2.at[lax.rem(q, 4)], g2_send.at[par], g2_recv.at[lax.rem(q, 4)],
            device_id=(me, sta ^ 2), device_id_type=MESH,
        )

    def g3_remote(q, par, m, target):
        ph = q // 8
        return pltpu.make_async_remote_copy(
            tx3.at[par, :, :, m],
            home.at[:, residue_of(ph, me), :, pl.ds(pl.multiple_of(16 * block_of(ph, me, m), 16), 16), :],
            g3_send.at[par, m], g3_recv.at[ph, m, me],
            device_id=(target, sta), device_id_type=MESH,
        )

    def g3_local(q, par, m):
        ph = q // 8
        return pltpu.make_async_copy(
            tx3.at[par, :, :, m],
            home.at[:, residue_of(ph, me), :, pl.ds(pl.multiple_of(16 * block_of(ph, me, m), 16), 16), :],
            g3_recv.at[ph, m, me],
        )

    def g3_arrived(ph, m, origin):
        return pltpu.make_async_remote_copy(
            tx3.at[0, :, :, m],
            home.at[:, residue_of(ph, origin), :, pl.ds(pl.multiple_of(16 * block_of(ph, origin, m), 16), 16), :],
            g3_send.at[0, m], g3_recv.at[ph, m, origin],
            device_id=(me, sta), device_id_type=MESH,
        )

    def stage1(q, par):
        for k in range(2):
            g1_remote(q, par, k).start()

    def stage2(q, par):
        for k in range(2):
            g1_remote(q, par, k).wait()

        @pl.when(q >= 2)
        def _():
            g2_remote(q - 2, par).wait_send()

        slot = lax.rem(q, 4)
        tx2[par] = gbuf[par, core + 2 * (1 - x)] + rx1[slot, 1 - x]
        keep2[par] = gbuf[par, core + 2 * x] + rx1[slot, x]
        g2_remote(q, par).start()

    def stage3(q, par):
        g2_remote(q, par).wait_recv()

        @pl.when(q >= 2)
        def _():
            finish3(q - 2, par)

        total = (keep2[par] + rx2[lax.rem(q, 4)]) * normalizer
        tx3[par] = total.reshape(tx3.shape[1:])
        target = lax.rem(q, 8)

        @pl.when(target == me)
        def _():
            for m in range(2):
                g3_local(q, par, m).start()

        @pl.when(target != me)
        def _():
            for m in range(2):
                g3_remote(q, par, m, target).start()

    def finish3(q, par):
        @pl.when(lax.rem(q, 8) == me)
        def _():
            for m in range(2):
                g3_local(q, par, m).wait()

        @pl.when(lax.rem(q, 8) != me)
        def _():
            for m in range(2):
                g3_remote(q, par, m, lax.rem(q, 8)).wait_send()

    def run_pair(q, par, cs, cs_next):
        ph, p = q // 8, lax.rem(q, 8)
        mem = member(ph)

        for e in range(2):
            @pl.when(q < 15)
            def _():
                own_copy(q + 1, 1 - par, e).start()

        @pl.when(4 + 2 * q < UNITS)
        def _():
            for k in range(2):
                send_unit(4 + 2 * q + k)

        for d in range(1, 4):
            y_remote(ph, p, d).wait_recv()
        for e in range(2):
            s_remote(ph, 2 * p + e).wait_recv()
            own_copy(q, par, e).wait()
        gbuf[par] = jnp.zeros_like(gbuf[par])

        def body(t, _):
            lanes = pl.ds(pl.multiple_of(t * TILE, TILE), TILE)
            rcats = []
            for e in range(2):
                at = 2 * q + e
                x1 = jnp.concatenate([x_all[s, at].reshape(64, 128) for s in range(4)], axis=1)
                x2 = jnp.concatenate([x1[32:], -x1[:32]], axis=0)
                both = jnp.concatenate([x1, x2], axis=1)
                acc = jnp.dot(x1, cs[e, t, :, 0:TILE], preferred_element_type=jnp.float32)
                acc += jnp.dot(x2, cs[e, t, :, TILE:], preferred_element_type=jnp.float32)
                acc = acc * normalizer
                seen = []
                for k in range(2):
                    mine = own[par, e, k, :, lanes]
                    theirs = spec_rx[ph, 2 * p + e, k, :, lanes].astype(jnp.float32)
                    seen.append(jnp.where(mem == 0, mine, theirs))
                    seen.append(jnp.where(mem == 0, theirs, mine))
                res = (acc - jnp.concatenate(seen, axis=0)).astype(jnp.bfloat16)
                rcats.append(jnp.concatenate([res, jnp.concatenate([-res[32:], res[:32]], axis=0)], axis=1))
            for e in range(2):
                back = lax.dot_general(rcats[e], cs[e, t], across, preferred_element_type=jnp.float32)
                for s in range(4):
                    gbuf[par, s, 64 * e : 64 * e + 64, :] += back[:, 128 * s : 128 * s + 128]
            for at in strips():
                row, col, _ = at
                store_pair(
                    (prev_cos[t, row, col], prev_sin[t, row, col]),
                    (now_cos[t, row, col], now_sin[t, row, col]),
                    chain[t, row, col], cs_next, t, at, first=False,
                )
            return 0

        lax.fori_loop(0, tiles, body, 0)

        @pl.when(q < 8)
        def _():
            forward(1, p)

        stage1(q, par)

        @pl.when(q >= 1)
        def _():
            stage2(q - 1, 1 - par)

        @pl.when(q >= 2)
        def _():
            stage3(q - 2, par)

    def two_pairs(i, _):
        run_pair(2 * i, 0, cs_a, cs_b)
        run_pair(2 * i + 1, 1, cs_b, cs_a)

        @pl.when(i == 3)
        def _():
            lax.fori_loop(0, tiles, again, 0)

        return 0

    lax.fori_loop(0, 8, two_pairs, 0)
    stage2(15, 1)
    stage3(14, 0)
    stage3(15, 1)

    for ph in range(2):
        for d in range(1, 8):
            for m in range(2):
                x_remote(ph, me ^ d, m, d, me).wait_send()
        for unit in range(UNITS - SBUF, UNITS):
            s_remote(ph, unit).wait_send()
    for ph in range(2):
        def left(origin, _):
            for d in range(1, 4):
                y_remote(ph, origin, d).wait_send()
            return 0

        lax.fori_loop(0, 8, left, 0)
    g2_remote(14, 0).wait_send()
    g2_remote(15, 1).wait_send()

    finish3(14, 0)
    finish3(15, 1)
    for ph in range(2):
        for d in range(1, 8):
            for m in range(2):
                g3_arrived(ph, m, me ^ d).wait_recv()

    def step_block(w, _):
        rows = pl.ds(pl.multiple_of(w * 16, 16), 16)
        total = jnp.zeros((16, 128), jnp.float32)
        for j in range(8):
            for k in range(2):
                value = current[j, k, rows, :] - step_size * home[j // 4, j % 4, k, rows, :]
                stepped_out[j, k, rows, :] = value
                total = total + value * value
        sums[0, w] = total
        return 0

    lax.fori_loop(0, 8, step_block, 0)

    def n_remote(d):
        return pltpu.make_async_remote_copy(
            sums.at[0, me ^ d], sums.at[1, d], n_send.at[d], n_recv.at[d],
            device_id=(me ^ d, sta), device_id_type=MESH,
        )

    for d in range(1, 8):
        n_remote(d).start()
    total = sums[0, me]
    for d in range(1, 8):
        n_remote(d).wait()
        total = total + sums[1, d]
    group_norm = jnp.sqrt(total + 1e-06)
    shrinks[me] = jnp.maximum(0.0, 1.0 - step_size * weights[...] / group_norm)

    def m_remote(d, slot):
        return pltpu.make_async_remote_copy(
            shrinks.at[slot], shrinks.at[slot], m_send.at[d], m_recv.at[d],
            device_id=(me ^ d, sta), device_id_type=MESH,
        )

    for d in range(1, 8):
        m_remote(d, me).start()
    for d in range(1, 8):
        m_remote(d, me).wait_send()
        m_remote(d, me ^ d).wait_recv()
    shrink_out[...] = shrinks[...].reshape(shrink_out.shape)


def local_paired(freq_size, sta_size, spectra, current, previous, table, station_block, offsets, slowness, weights, momentum):
    period = 4 * F
    normalizer = 1.0 / math.sqrt(CELLS)
    bins, _, windows, share = current.shape
    stations = station_block.shape[0]
    cells = table.shape[1]
    step_size = CELLS / (math.sqrt(stations * sta_size) + math.sqrt(CELLS)) ** 2
    tiles = stations // TILE
    f32, bf16 = jnp.float32, jnp.bfloat16
    vm, dma = pltpu.VMEM, pltpu.SemaphoreType.DMA
    state = vm((tiles, cells, TILE), f32)
    piece = spectra.shape[1]
    slow = jnp.pad(slowness, ((0, 6), (0, 0)))
    inside = pl.BlockSpec(memory_space=pltpu.VMEM)
    stepped, shrink = pl.pallas_call(
        functools.partial(iteration_kernel, period, normalizer, step_size),
        out_shape=(
            jax.ShapeDtypeStruct((bins, 2, windows, share), f32),
            jax.ShapeDtypeStruct((windows, share), f32),
        ),
        in_specs=[pl.BlockSpec(memory_space=pl.ANY)] + [inside] * 6,
        out_specs=(inside, inside),
        scratch_shapes=[
            vm((2, tiles, cells, 2 * TILE), bf16),
            vm((2, tiles, cells, 2 * TILE), bf16),
            state, state, state, state, state, state, state,
            vm((cells, table.shape[0]), bf16),
            vm((cells, 8), f32),
            vm((cells, TILE), f32),
            vm((2, 4, 2, windows, share), bf16),
            vm((4, 32, 2, 32, share), bf16),
            vm((2, UNITS, 2, piece, stations), bf16),
            vm((2, SBUF, 2, piece, stations), bf16),
            vm((2, STAGE, 2, piece, stations), f32),
            vm((2, 2, 2, piece, stations), f32),
            vm((2, 4, 2, windows, share), f32),
            vm((2, 4, 128, share), f32),
            vm((4, 2, 128, share), f32),
            vm((4, 128, share), f32),
            vm((2, 128, share), f32),
            vm((2, 128, share), f32),
            vm((2, 2, 2, 2, 16, share), f32),
            vm((2, 8, 16, share), f32),
            vm((8, 16, share), f32),
            dma((2, 2, 8)), dma((2, 2, 8)), dma((2, 8, 4)), dma((2, 8, 4)),
            dma((2, SBUF)), dma((2, UNITS)), dma((2, STAGE)), dma((2, 2)),
            dma((2, 2)), dma((4, 2)), dma((2,)), dma((4,)), dma((2, 2)), dma((2, 2, 8)),
            dma((8,)), dma((8,)), dma((8,)), dma((8,)),
        ],
        compiler_params=pltpu.CompilerParams(
            vmem_limit_bytes=63 * 2**20, collective_id=0, has_side_effects=True
        ),
        cost_estimate=pl.CostEstimate(
            flops=8 * 32 * 64 * cells * stations, bytes_accessed=24 * 2**20, transcendentals=0
        ),
    )(spectra, current, table, station_block.reshape(1, -1), offsets, slow, weights.reshape(1, -1))
    estimate = stepped * shrink
    momentum_now = momentum[0]
    momentum_next = (1.0 + jnp.sqrt(1.0 + 4.0 * momentum_now * momentum_now)) / 2.0
    extrapolated = estimate + (momentum_now - 1.0) / momentum_next * (estimate - previous)
    return (estimate, extrapolated)


def solution(mesh):
    freq_size, sta_size = mesh.shape["freq"], mesh.shape["sta"]
    body = local
    if freq_size == 8 and sta_size == 4:
        body = functools.partial(local_paired, freq_size, sta_size)
    in_specs = (
        P(None, "freq", None, "sta"),
        P("freq", None, None, "sta"),
        P("freq", None, None, "sta"),
        P(),
        P("sta"),
        P(None, "sta"),
        P(),
        P("sta"),
        P(),
    )
    out_specs = (P("freq", None, None, "sta"), P("freq", None, None, "sta"))
    return jax.shard_map(body, mesh=mesh, in_specs=in_specs, out_specs=out_specs, check_vma=False)
```

```python
import functools
import math

import jax
import jax.numpy as jnp
from jax import lax
from jax.experimental import pallas as pl
from jax.experimental.pallas import tpu as pltpu
from jax.sharding import PartitionSpec as P

F = 64
CELLS = 512


def cell_block(cell_count):
    block_len = cell_count
    while block_len > 512 and block_len % 2 == 0:
        block_len = block_len // 2
    return block_len


def phases(number, delay_rows, off_rows, slow_cols, period):
    wrapped = number * delay_rows % period
    geometry = (
        off_rows[0][:, None] * slow_cols[0][None, :] + off_rows[1][:, None] * slow_cols[1][None, :]
    )
    phase_angle = (wrapped.astype(jnp.float32) + number.astype(jnp.float32) * geometry) * (
        2.0 * math.pi / period
    )
    return (jnp.cos(phase_angle).astype(jnp.bfloat16), jnp.sin(phase_angle).astype(jnp.bfloat16))


def forward_terms(cos_part, sin_part, iterate):
    window_count = iterate.shape[1]
    stacked = iterate.reshape(2 * window_count, iterate.shape[2])
    contract = (((1,), (1,)), ((), ()))
    with_cos = lax.dot_general(stacked, cos_part, contract, preferred_element_type=jnp.float32)
    with_sin = lax.dot_general(stacked, sin_part, contract, preferred_element_type=jnp.float32)
    real_part = with_cos[:window_count] + with_sin[window_count:]
    imag_part = with_cos[window_count:] - with_sin[:window_count]
    return jnp.stack([real_part, imag_part])


def adjoint_terms(cos_part, sin_part, residual):
    window_count = residual.shape[1]
    stacked = residual.reshape(2 * window_count, residual.shape[2])
    with_cos = jnp.dot(stacked, cos_part, preferred_element_type=jnp.float32)
    with_sin = jnp.dot(stacked, sin_part, preferred_element_type=jnp.float32)
    real_part = with_cos[:window_count] - with_sin[window_count:]
    imag_part = with_cos[window_count:] + with_sin[:window_count]
    return jnp.stack([real_part, imag_part])


def local(spectra, current, previous, table, station_block, offsets, slowness, weights, momentum):
    period = 4 * F
    normalizer = 1.0 / math.sqrt(CELLS)
    bin_count = current.shape[0]
    cell_share = current.shape[3]
    stations_here = station_block.shape[0]
    station_total = stations_here * lax.axis_size("sta")
    first_bin = lax.axis_index("freq") * bin_count
    relaid = lax.all_to_all(
        spectra.astype(jnp.bfloat16), "freq", split_axis=2, concat_axis=1, tiled=True
    ).astype(spectra.dtype)
    iterate_b = current.astype(jnp.bfloat16)
    segment = lax.all_gather(iterate_b, "sta", axis=3, tiled=True)
    cell_count = segment.shape[3]
    block_len = cell_block(cell_count)
    delay_rows = jnp.take(table, station_block, axis=0)
    bin_terms = []
    cos_blocks = []
    sin_blocks = []
    for add_bin_index in range(bin_count):
        cos_part, sin_part = phases(
            first_bin + add_bin_index + 1, delay_rows, offsets, slowness, period
        )
        cos_blocks.append(cos_part)
        sin_blocks.append(sin_part)
        bin_terms.append(
            forward_terms(cos_part, sin_part, segment[add_bin_index, :, :, 0:block_len])
        )
    running = jnp.stack(bin_terms)
    cos_all = jnp.stack(cos_blocks)
    sin_all = jnp.stack(sin_blocks)
    predicted, cos_all, sin_all = (running, cos_all, sin_all)
    bin_sums = []
    for bin_index in range(bin_count):
        residual = (predicted[bin_index] * normalizer - relaid[:, :, bin_index, :]).astype(
            jnp.bfloat16
        )
        bin_sums.append(
            adjoint_terms(cos_all[bin_index], sin_all[bin_index], residual) * normalizer
        )
    partial_sums = jnp.stack(bin_sums)
    summed = lax.psum(partial_sums, "sta")
    gradient = lax.dynamic_slice_in_dim(summed, lax.axis_index("sta") * cell_share, cell_share, 3)
    step_size = CELLS / (math.sqrt(station_total) + math.sqrt(CELLS)) ** 2
    stepped = current - step_size * gradient
    threshold = step_size * weights
    squares = jnp.sum(stepped * stepped, axis=(0, 1))
    group_norm = jnp.sqrt(lax.psum(squares, "freq") + 1e-06)
    estimate = stepped * jnp.maximum(0.0, 1.0 - threshold[None, :] / group_norm)
    momentum_now = momentum[0]
    momentum_next = (1.0 + jnp.sqrt(1.0 + 4.0 * momentum_now * momentum_now)) / 2.0
    extrapolated = estimate + (momentum_now - 1.0) / momentum_next * (estimate - previous)
    return (estimate, extrapolated)


SIN_TERMS = (3.1415926535362892, -5.167712764624382, 2.5501633189428987, -0.5992521977810126, 0.08205040162239277, -0.007028386120383206)
COS_TERMS = (0.9999999997799041, -4.934802137078749, 4.058709159554242, -1.335212003029471, 0.23493731372678894, -0.024396324214549327)
MESH = pl.DeviceIdType.MESH
TILE = 512
ROWS = 32
COLS = 256
UNITS = 16
STRIP = 16
SBUF = 4
STAGE = 2


def horner(terms, u):
    total = jnp.full_like(u, terms[-1])
    for term in terms[-2::-1]:
        total = total * u + term
    return total


def turns_cos_sin(turns):
    part = turns - jnp.round(turns)
    square = part * part
    half_sin = part * horner(SIN_TERMS, square)
    half_cos = horner(COS_TERMS, square)
    doubled = half_sin + half_sin
    return 1.0 - doubled * half_sin, doubled * half_cos


def times(a, b):
    return a[0] * b[0] - a[1] * b[1], a[1] * b[0] + a[0] * b[1]


def twice(a):
    doubled = a[1] + a[1]
    return 1.0 - doubled * a[1], doubled * a[0]


def iteration_kernel(
    period, normalizer, step_size,
    spectra, current_in, table, blocks, offsets, slowness, weights,
    stepped_out, shrink_out,
    cs_a, cs_b, prev_cos, prev_sin, now_cos, now_sin, unit_cos, unit_sin, chain,
    tab_t, slow_8, slow_t, delay, current,
    current_b, x_all, spec_rx, sbuf, stage, own, home, gbuf, rx1, rx2, tx2, keep2, tx3, sums, shrinks,
    x_send, x_recv, y_send, y_recv, s_send, s_recv, l_stage, l_own,
    g1_send, g1_recv, g2_send, g2_recv, g3_send, g3_recv, n_send, n_recv, m_send, m_recv, l_current,
):
    me = lax.axis_index("freq")
    sta = lax.axis_index("sta")
    z, y = me // 2, me % 2
    zl, zp = z % 2, z // 2
    x, core = sta // 2, sta % 2
    tiles = cs_a.shape[1]

    def pick(ph, first, second):
        return jnp.where(ph == 0, first, second)

    def block_of(ph, fd, m):
        return pick(ph, fd // 2 * 2 + m, (fd // 4 * 2 + m) * 2 + fd % 2)

    def residue_of(ph, fd):
        return pick(ph, 2 * (fd % 2), 1 + 2 * (fd // 2 % 2))

    def member(ph):
        return pick(ph, y, zl)

    def partner(ph):
        return pick(ph, me ^ 1, me ^ 2)

    def stage_copy(ph, unit):
        slot = lax.rem(unit, STAGE)
        line = 4 * unit + residue_of(ph, partner(ph))
        return pltpu.make_async_copy(spectra.at[:, :, line, :], stage.at[ph, slot], l_stage.at[ph, slot])

    def own_copy(q, par, e):
        ph = q // 8
        line = 4 * (2 * (q % 8) + e) + residue_of(ph, me)
        return pltpu.make_async_copy(spectra.at[:, :, line, :], own.at[par, e], l_own.at[par, e])

    load = pltpu.make_async_copy(current_in, current, l_current)
    load.start()
    barrier = pltpu.get_barrier_semaphore()
    for d in range(1, 8):
        pl.semaphore_signal(barrier, inc=1, device_id=(me ^ d, sta), device_id_type=MESH)
    for d in range(1, 4):
        pl.semaphore_signal(barrier, inc=1, device_id=(me, sta ^ d), device_id_type=MESH)
    load.wait()
    for first in range(STAGE):
        for ph in range(2):
            stage_copy(ph, first).start()
    for e in range(2):
        own_copy(0, 0, e).start()
    for j in range(8):
        current_b[j // 4, j % 4] = current[j].astype(jnp.bfloat16)
    pl.semaphore_wait(barrier, 10)

    def x_remote(ph, fd, m, source, origin):
        return pltpu.make_async_remote_copy(
            current_b.at[:, residue_of(ph, fd), :, pl.ds(pl.multiple_of(16 * block_of(ph, fd, m), 16), 16), :],
            x_all.at[sta, pl.ds(8 * 2 * ph + 2 * origin, 2), :, pl.ds(16 * m, 16), :],
            x_send.at[ph, m, source], x_recv.at[ph, m, origin],
            device_id=(fd, sta), device_id_type=MESH,
        )

    def x_local(ph, m):
        return pltpu.make_async_copy(
            current_b.at[:, residue_of(ph, me), :, pl.ds(pl.multiple_of(16 * block_of(ph, me, m), 16), 16), :],
            x_all.at[sta, pl.ds(8 * 2 * ph + 2 * me, 2), :, pl.ds(16 * m, 16), :],
            x_recv.at[ph, m, me],
        )

    for ph in range(2):
        for m in range(2):
            x_local(ph, m).start()
        for d in range(1, 8):
            for m in range(2):
                x_remote(ph, me ^ d, m, d, me).start()

    def forward(ph, origin):
        for m in range(2):
            @pl.when(origin == me)
            def _():
                x_local(ph, m).wait()

            @pl.when(origin != me)
            def _():
                x_remote(ph, me, m, 1, origin).wait_recv()
        for d in range(1, 3):
            y_remote(ph, origin, d).start()

    def y_remote(ph, origin, d):
        rows = pl.ds(16 * ph + 2 * origin, 2)
        held = sta ^ 2 if d == 3 else sta
        return pltpu.make_async_remote_copy(
            x_all.at[held, rows], x_all.at[held, rows],
            y_send.at[ph, origin, d], y_recv.at[ph, origin, d],
            device_id=(me, sta ^ (2 if d == 2 else 1)), device_id_type=MESH,
        )

    def relay(q):
        ph, origin = q // 8, lax.rem(q, 8)
        y_remote(ph, origin, 2).wait_recv()
        y_remote(ph, origin, 3).start()

    def s_remote(ph, unit):
        slot = lax.rem(unit, SBUF)
        return pltpu.make_async_remote_copy(
            sbuf.at[ph, slot], spec_rx.at[ph, unit], s_send.at[ph, slot], s_recv.at[ph, unit],
            device_id=(partner(ph), sta), device_id_type=MESH,
        )

    def send_unit(ph, unit):
        stage_copy(ph, unit).wait()

        @pl.when(unit >= SBUF)
        def _():
            s_remote(ph, unit - SBUF).wait_send()

        sbuf[ph, lax.rem(unit, SBUF)] = stage[ph, lax.rem(unit, STAGE)].astype(jnp.bfloat16)
        s_remote(ph, unit).start()

        @pl.when(unit + STAGE < UNITS)
        def _():
            stage_copy(ph, unit + STAGE).start()

    tab_t[...] = jnp.transpose(jnp.bitwise_and(table[...], period - 1).astype(jnp.float32)).astype(jnp.bfloat16)
    slow_8[...] = jnp.zeros_like(slow_8)
    slow_8[0:2, :] = slowness[...]
    slow_t[...] = jnp.transpose(slow_8[...])
    cells = delay.shape[0]
    scale = 1.0 / period

    def start_chain(ph, unit, turn, cs, t, at):
        second = twice(unit)
        if ph == 0:
            third = times(unit, second)
            a = jnp.where(y == 0, third[0], unit[0]), -jnp.where(y == 0, third[1], unit[1])
            b = jnp.where(y == 0, unit[0], third[0]), jnp.where(y == 0, unit[1], third[1])
        else:
            fourth = twice(second)
            a = jnp.where(zl == 0, second[0], 1.0), jnp.where(zl == 0, -second[1], 0.0)
            b = jnp.where(zl == 0, second[0], fourth[0]), jnp.where(zl == 0, second[1], fourth[1])
        return store_pair(a, b, turn, cs, t, at, True)

    def store_pair(a, b, turn, cs, t, at, first):
        row, col, col_s = at
        one = b if first else (turn * b[0] - a[0], turn * b[1] - a[1])
        old = a if first else b
        two = turn * one[0] - old[0], turn * one[1] - old[1]
        prev_cos[t, row, col], prev_sin[t, row, col] = one
        now_cos[t, row, col], now_sin[t, row, col] = two
        for e, value in enumerate((one, two)):
            cs[e, t, row, col] = value[0].astype(jnp.bfloat16)
            cs[e, t, row, col_s] = value[1].astype(jnp.bfloat16)
        return two[0]

    def fill(cs, t, fresh):
        after = None
        for r in range(0, cells, STRIP):
            for c in range(0, TILE, 128):
                row, col, col_s = slice(r, r + STRIP), slice(c, c + 128), slice(TILE + c, TILE + c + 128)
                turn = chain[t, row, col]
                if after is not None:
                    turn = turn + after
                at = row, col, col_s
                if fresh:
                    unit = unit_cos[t, row, col], unit_sin[t, row, col]
                    if after is not None:
                        unit = unit[0] + after, unit[1]
                    last = start_chain(1, unit, turn, cs, t, at)
                else:
                    old = prev_cos[t, row, col], prev_sin[t, row, col]
                    now = now_cos[t, row, col], now_sin[t, row, col]
                    last = store_pair(old, now, turn, cs, t, at, False)
                zero = jnp.minimum(jnp.maximum(last[0:8], 0.0), 0.0)
                after = jnp.concatenate([zero] * (STRIP // 8), axis=0)

    def angles(t, _):
        lanes = pl.ds(pl.multiple_of(t * TILE, TILE), TILE)
        picks = lax.broadcasted_iota(jnp.int32, (tab_t.shape[1], TILE), 0)
        picks = jnp.where(picks == blocks[:, lanes], 1.0, 0.0).astype(jnp.bfloat16)
        delay[...] = jnp.dot(tab_t[...], picks, preferred_element_type=jnp.float32)

        def strip(index, _):
            r = pl.multiple_of(index * ROWS, ROWS)
            row = pl.ds(r, ROWS)
            slow = slow_t[row, :]
            for c in range(0, TILE, COLS):
                col, col_s = slice(c, c + COLS), slice(TILE + c, TILE + c + COLS)
                here = pl.ds(pl.multiple_of(t * TILE + c, COLS), COLS)
                geometry = offsets[0:1, here] * slow[:, 0:1] + offsets[1:2, here] * slow[:, 1:2]
                turns = delay[row, col] * scale
                unit = turns_cos_sin((delay[row, col] + geometry) * scale)
                turns = 4.0 * turns
                fourth, _ = turns_cos_sin((turns - jnp.round(turns)) + geometry * (4.0 * scale))
                turn = fourth + fourth
                unit_cos[t, row, col], unit_sin[t, row, col] = unit
                chain[t, row, col] = turn
                start_chain(0, unit, turn, cs_a, t, (row, col, col_s))
            return 0

        lax.fori_loop(0, cells // ROWS, strip, 0)
        send_unit(0, t)

        @pl.when(t >= 2)
        def _():
            for k in range(4):
                forward(0, 4 * (t - 2) + k)

        return 0

    lax.fori_loop(0, tiles, angles, 0)

    across = (((1,), (1,)), ((), ()))

    def g1_remote(q, par, k):
        share = 1 - core + 2 * k
        return pltpu.make_async_remote_copy(
            gbuf.at[par, share], rx1.at[lax.rem(q, 4), k], g1_send.at[par, k], g1_recv.at[lax.rem(q, 4), k],
            device_id=(me, sta ^ 1), device_id_type=MESH,
        )

    def g2_remote(q, par):
        return pltpu.make_async_remote_copy(
            tx2.at[par], rx2.at[lax.rem(q, 4)], g2_send.at[par], g2_recv.at[lax.rem(q, 4)],
            device_id=(me, sta ^ 2), device_id_type=MESH,
        )

    def g3_remote(q, m, target):
        ph = q // 8
        return pltpu.make_async_remote_copy(
            tx3.at[lax.rem(q, 8), :, :, m],
            home.at[:, residue_of(ph, me), :, pl.ds(pl.multiple_of(16 * block_of(ph, me, m), 16), 16), :],
            g3_send.at[lax.rem(q, 8), m], g3_recv.at[ph, m, me],
            device_id=(target, sta), device_id_type=MESH,
        )

    def g3_local(q, m):
        ph = q // 8
        return pltpu.make_async_copy(
            tx3.at[lax.rem(q, 8), :, :, m],
            home.at[:, residue_of(ph, me), :, pl.ds(pl.multiple_of(16 * block_of(ph, me, m), 16), 16), :],
            g3_recv.at[ph, m, me],
        )

    def g3_arrived(ph, m, origin):
        return pltpu.make_async_remote_copy(
            tx3.at[0, :, :, m],
            home.at[:, residue_of(ph, origin), :, pl.ds(pl.multiple_of(16 * block_of(ph, origin, m), 16), 16), :],
            g3_send.at[0, m], g3_recv.at[ph, m, origin],
            device_id=(me, sta), device_id_type=MESH,
        )

    def stage1(q, par):
        for k in range(2):
            g1_remote(q, par, k).start()

    def stage2(q, par):
        for k in range(2):
            g1_remote(q, par, k).wait()

        @pl.when(q >= 2)
        def _():
            g2_remote(q - 2, par).wait_send()

        slot = lax.rem(q, 4)
        tx2[par] = gbuf[par, core + 2 * (1 - x)] + rx1[slot, 1 - x]
        keep2[par] = gbuf[par, core + 2 * x] + rx1[slot, x]
        g2_remote(q, par).start()

    def stage3(q, par):
        g2_remote(q, par).wait_recv()

        @pl.when(q >= 8)
        def _():
            finish3(q - 8)

        total = (keep2[par] + rx2[lax.rem(q, 4)]) * normalizer
        target = lax.rem(q, 8)
        tx3[target] = total.reshape(tx3.shape[1:])

        @pl.when(target == me)
        def _():
            for m in range(2):
                g3_local(q, m).start()

        @pl.when(target != me)
        def _():
            for m in range(2):
                g3_remote(q, m, target).start()

    def finish3(q):
        @pl.when(lax.rem(q, 8) == me)
        def _():
            for m in range(2):
                g3_local(q, m).wait()

        @pl.when(lax.rem(q, 8) != me)
        def _():
            for m in range(2):
                g3_remote(q, m, lax.rem(q, 8)).wait_send()

    def run_pair(q, par, cs, cs_next):
        ph, p = q // 8, lax.rem(q, 8)
        mem = member(ph)

        for e in range(2):
            @pl.when(q < 15)
            def _():
                own_copy(q + 1, 1 - par, e).start()

        @pl.when(4 + 2 * q < UNITS)
        def _():
            for k in range(2):
                send_unit(0, 4 + 2 * q + k)

        @pl.when(2 * q < UNITS)
        def _():
            for k in range(2):
                send_unit(1, 2 * q + k)

        @pl.when(q < 15)
        def _():
            relay(q + 1)

        y_remote(ph, p, 1).wait_recv()
        y_remote(ph, p, 3).wait_recv()
        for e in range(2):
            s_remote(ph, 2 * p + e).wait_recv()
            own_copy(q, par, e).wait()
        gbuf[par] = jnp.zeros_like(gbuf[par])

        def body(mode, t, _):
            lanes = pl.ds(pl.multiple_of(t * TILE, TILE), TILE)
            rcats = []
            for e in range(2):
                at = 2 * q + e
                x1 = jnp.concatenate([x_all[s, at].reshape(64, 128) for s in range(4)], axis=1)
                x2 = jnp.concatenate([x1[32:], -x1[:32]], axis=0)
                acc = jnp.dot(x1, cs[e, t, :, 0:TILE], preferred_element_type=jnp.float32)
                acc += jnp.dot(x2, cs[e, t, :, TILE:], preferred_element_type=jnp.float32)
                acc = acc * normalizer
                seen = []
                for k in range(2):
                    mine = own[par, e, k, :, lanes]
                    theirs = spec_rx[ph, 2 * p + e, k, :, lanes].astype(jnp.float32)
                    seen.append(jnp.where(mem == 0, mine, theirs))
                    seen.append(jnp.where(mem == 0, theirs, mine))
                res = (acc - jnp.concatenate(seen, axis=0)).astype(jnp.bfloat16)
                rcats.append(jnp.concatenate([res, jnp.concatenate([-res[32:], res[:32]], axis=0)], axis=1))
            for e in range(2):
                back = lax.dot_general(rcats[e], cs[e, t], across, preferred_element_type=jnp.float32)
                for s in range(4):
                    gbuf[par, s, 64 * e : 64 * e + 64, :] += back[:, 128 * s : 128 * s + 128]
            if mode != "none":
                fill(cs_next, t, mode == "fresh")
            return 0

        if par == 0:
            lax.fori_loop(0, tiles, functools.partial(body, "next"), 0)
        else:
            for mode, here in (("fresh", q == 7), ("none", q == 15), ("next", (q != 7) & (q != 15))):
                @pl.when(here)
                def _():
                    lax.fori_loop(0, tiles, functools.partial(body, mode), 0)

        @pl.when(q < 8)
        def _():
            forward(1, p)

        stage1(q, par)

        @pl.when(q >= 1)
        def _():
            stage2(q - 1, 1 - par)

        @pl.when(q >= 2)
        def _():
            stage3(q - 2, par)

    def two_pairs(i, _):
        run_pair(2 * i, 0, cs_a, cs_b)
        run_pair(2 * i + 1, 1, cs_b, cs_a)
        return 0

    relay(0)
    lax.fori_loop(0, 8, two_pairs, 0)
    stage2(15, 1)
    stage3(14, 0)
    stage3(15, 1)

    for ph in range(2):
        for d in range(1, 8):
            for m in range(2):
                x_remote(ph, me ^ d, m, d, me).wait_send()
        for unit in range(UNITS - SBUF, UNITS):
            s_remote(ph, unit).wait_send()
    for ph in range(2):
        def left(origin, _):
            for d in range(1, 4):
                y_remote(ph, origin, d).wait_send()
            return 0

        lax.fori_loop(0, 8, left, 0)
    g2_remote(14, 0).wait_send()
    g2_remote(15, 1).wait_send()

    def finished(q, _):
        finish3(q)
        return 0

    lax.fori_loop(8, 16, finished, 0)
    for ph in range(2):
        for d in range(1, 8):
            for m in range(2):
                g3_arrived(ph, m, me ^ d).wait_recv()

    def step_block(w, _):
        rows = pl.ds(pl.multiple_of(w * 16, 16), 16)
        total = jnp.zeros((16, 128), jnp.float32)
        for j in range(8):
            for k in range(2):
                value = current[j, k, rows, :] - step_size * home[j // 4, j % 4, k, rows, :]
                stepped_out[j, k, rows, :] = value
                total = total + value * value
        sums[0, w] = total
        return 0

    lax.fori_loop(0, 8, step_block, 0)

    def n_remote(d):
        return pltpu.make_async_remote_copy(
            sums.at[0, me ^ d], sums.at[1, d], n_send.at[d], n_recv.at[d],
            device_id=(me ^ d, sta), device_id_type=MESH,
        )

    for d in range(1, 8):
        n_remote(d).start()
    total = sums[0, me]
    for d in range(1, 8):
        n_remote(d).wait()
        total = total + sums[1, d]
    group_norm = jnp.sqrt(total + 1e-06)
    shrinks[me] = jnp.maximum(0.0, 1.0 - step_size * weights[...] / group_norm)

    def m_remote(d, slot):
        return pltpu.make_async_remote_copy(
            shrinks.at[slot], shrinks.at[slot], m_send.at[d], m_recv.at[d],
            device_id=(me ^ d, sta), device_id_type=MESH,
        )

    for d in range(1, 8):
        m_remote(d, me).start()
    for d in range(1, 8):
        m_remote(d, me).wait_send()
        m_remote(d, me ^ d).wait_recv()
    shrink_out[...] = shrinks[...].reshape(shrink_out.shape)


def local_paired(freq_size, sta_size, spectra, current, previous, table, station_block, offsets, slowness, weights, momentum):
    period = 4 * F
    normalizer = 1.0 / math.sqrt(CELLS)
    bins, _, windows, share = current.shape
    stations = station_block.shape[0]
    cells = table.shape[1]
    step_size = CELLS / (math.sqrt(stations * sta_size) + math.sqrt(CELLS)) ** 2
    tiles = stations // TILE
    f32, bf16 = jnp.float32, jnp.bfloat16
    vm, dma = pltpu.VMEM, pltpu.SemaphoreType.DMA
    state = vm((tiles, cells, TILE), f32)
    piece = spectra.shape[1]
    inside = pl.BlockSpec(memory_space=pltpu.VMEM)
    stepped, shrink = pl.pallas_call(
        functools.partial(iteration_kernel, period, normalizer, step_size),
        out_shape=(
            jax.ShapeDtypeStruct((bins, 2, windows, share), f32),
            jax.ShapeDtypeStruct((windows, share), f32),
        ),
        in_specs=[pl.BlockSpec(memory_space=pl.ANY)] * 2 + [inside] * 5,
        out_specs=(inside, inside),
        scratch_shapes=[
            vm((2, tiles, cells, 2 * TILE), bf16),
            vm((2, tiles, cells, 2 * TILE), bf16),
            state, state, state, state, state, state, state,
            vm((cells, table.shape[0]), bf16),
            vm((8, cells), f32),
            vm((cells, 8), f32),
            vm((cells, TILE), f32),
            vm(current.shape, f32),
            vm((2, 4, 2, windows, share), bf16),
            vm((4, 32, 2, 32, share), bf16),
            vm((2, UNITS, 2, piece, stations), bf16),
            vm((2, SBUF, 2, piece, stations), bf16),
            vm((2, STAGE, 2, piece, stations), f32),
            vm((2, 2, 2, piece, stations), f32),
            vm((2, 4, 2, windows, share), f32),
            vm((2, 4, 128, share), f32),
            vm((4, 2, 128, share), f32),
            vm((4, 128, share), f32),
            vm((2, 128, share), f32),
            vm((2, 128, share), f32),
            vm((8, 2, 2, 2, 16, share), f32),
            vm((2, 8, 16, share), f32),
            vm((8, 16, share), f32),
            dma((2, 2, 8)), dma((2, 2, 8)), dma((2, 8, 4)), dma((2, 8, 4)),
            dma((2, SBUF)), dma((2, UNITS)), dma((2, STAGE)), dma((2, 2)),
            dma((2, 2)), dma((4, 2)), dma((2,)), dma((4,)), dma((8, 2)), dma((2, 2, 8)),
            dma((8,)), dma((8,)), dma((8,)), dma((8,)), dma(()),
        ],
        compiler_params=pltpu.CompilerParams(
            vmem_limit_bytes=63 * 2**20, collective_id=0, has_side_effects=True
        ),
        cost_estimate=pl.CostEstimate(
            flops=8 * 32 * 64 * cells * stations, bytes_accessed=24 * 2**20, transcendentals=0
        ),
    )(spectra, current, table, station_block.reshape(1, -1), offsets, slowness, weights.reshape(1, -1))
    estimate = stepped * shrink
    momentum_now = momentum[0]
    momentum_next = (1.0 + jnp.sqrt(1.0 + 4.0 * momentum_now * momentum_now)) / 2.0
    extrapolated = estimate + (momentum_now - 1.0) / momentum_next * (estimate - previous)
    return (estimate, extrapolated)


def solution(mesh):
    freq_size, sta_size = mesh.shape["freq"], mesh.shape["sta"]
    body = local
    if freq_size == 8 and sta_size == 4:
        body = functools.partial(local_paired, freq_size, sta_size)
    in_specs = (
        P(None, "freq", None, "sta"),
        P("freq", None, None, "sta"),
        P("freq", None, None, "sta"),
        P(),
        P("sta"),
        P(None, "sta"),
        P(),
        P("sta"),
        P(),
    )
    out_specs = (P("freq", None, None, "sta"), P("freq", None, None, "sta"))
    return jax.shard_map(body, mesh=mesh, in_specs=in_specs, out_specs=out_specs, check_vma=False)
```

```python
import functools
import math

import jax
import jax.numpy as jnp
from jax import lax
from jax.experimental import pallas as pl
from jax.experimental.pallas import tpu as pltpu
from jax.sharding import PartitionSpec as P

F = 64
CELLS = 512


def cell_block(cell_count):
    block_len = cell_count
    while block_len > 512 and block_len % 2 == 0:
        block_len = block_len // 2
    return block_len


def phases(number, delay_rows, off_rows, slow_cols, period):
    wrapped = number * delay_rows % period
    geometry = (
        off_rows[0][:, None] * slow_cols[0][None, :] + off_rows[1][:, None] * slow_cols[1][None, :]
    )
    phase_angle = (wrapped.astype(jnp.float32) + number.astype(jnp.float32) * geometry) * (
        2.0 * math.pi / period
    )
    return (jnp.cos(phase_angle).astype(jnp.bfloat16), jnp.sin(phase_angle).astype(jnp.bfloat16))


def forward_terms(cos_part, sin_part, iterate):
    window_count = iterate.shape[1]
    stacked = iterate.reshape(2 * window_count, iterate.shape[2])
    contract = (((1,), (1,)), ((), ()))
    with_cos = lax.dot_general(stacked, cos_part, contract, preferred_element_type=jnp.float32)
    with_sin = lax.dot_general(stacked, sin_part, contract, preferred_element_type=jnp.float32)
    real_part = with_cos[:window_count] + with_sin[window_count:]
    imag_part = with_cos[window_count:] - with_sin[:window_count]
    return jnp.stack([real_part, imag_part])


def adjoint_terms(cos_part, sin_part, residual):
    window_count = residual.shape[1]
    stacked = residual.reshape(2 * window_count, residual.shape[2])
    with_cos = jnp.dot(stacked, cos_part, preferred_element_type=jnp.float32)
    with_sin = jnp.dot(stacked, sin_part, preferred_element_type=jnp.float32)
    real_part = with_cos[:window_count] - with_sin[window_count:]
    imag_part = with_cos[window_count:] + with_sin[:window_count]
    return jnp.stack([real_part, imag_part])


def local(spectra, current, previous, table, station_block, offsets, slowness, weights, momentum):
    period = 4 * F
    normalizer = 1.0 / math.sqrt(CELLS)
    bin_count = current.shape[0]
    cell_share = current.shape[3]
    stations_here = station_block.shape[0]
    station_total = stations_here * lax.axis_size("sta")
    first_bin = lax.axis_index("freq") * bin_count
    relaid = lax.all_to_all(
        spectra.astype(jnp.bfloat16), "freq", split_axis=2, concat_axis=1, tiled=True
    ).astype(spectra.dtype)
    iterate_b = current.astype(jnp.bfloat16)
    segment = lax.all_gather(iterate_b, "sta", axis=3, tiled=True)
    cell_count = segment.shape[3]
    block_len = cell_block(cell_count)
    delay_rows = jnp.take(table, station_block, axis=0)
    bin_terms = []
    cos_blocks = []
    sin_blocks = []
    for add_bin_index in range(bin_count):
        cos_part, sin_part = phases(
            first_bin + add_bin_index + 1, delay_rows, offsets, slowness, period
        )
        cos_blocks.append(cos_part)
        sin_blocks.append(sin_part)
        bin_terms.append(
            forward_terms(cos_part, sin_part, segment[add_bin_index, :, :, 0:block_len])
        )
    running = jnp.stack(bin_terms)
    cos_all = jnp.stack(cos_blocks)
    sin_all = jnp.stack(sin_blocks)
    predicted, cos_all, sin_all = (running, cos_all, sin_all)
    bin_sums = []
    for bin_index in range(bin_count):
        residual = (predicted[bin_index] * normalizer - relaid[:, :, bin_index, :]).astype(
            jnp.bfloat16
        )
        bin_sums.append(
            adjoint_terms(cos_all[bin_index], sin_all[bin_index], residual) * normalizer
        )
    partial_sums = jnp.stack(bin_sums)
    summed = lax.psum(partial_sums, "sta")
    gradient = lax.dynamic_slice_in_dim(summed, lax.axis_index("sta") * cell_share, cell_share, 3)
    step_size = CELLS / (math.sqrt(station_total) + math.sqrt(CELLS)) ** 2
    stepped = current - step_size * gradient
    threshold = step_size * weights
    squares = jnp.sum(stepped * stepped, axis=(0, 1))
    group_norm = jnp.sqrt(lax.psum(squares, "freq") + 1e-06)
    estimate = stepped * jnp.maximum(0.0, 1.0 - threshold[None, :] / group_norm)
    momentum_now = momentum[0]
    momentum_next = (1.0 + jnp.sqrt(1.0 + 4.0 * momentum_now * momentum_now)) / 2.0
    extrapolated = estimate + (momentum_now - 1.0) / momentum_next * (estimate - previous)
    return (estimate, extrapolated)


SIN_TERMS = (3.1415926535362892, -5.167712764624382, 2.5501633189428987, -0.5992521977810126, 0.08205040162239277, -0.007028386120383206)
COS_TERMS = (0.9999999997799041, -4.934802137078749, 4.058709159554242, -1.335212003029471, 0.23493731372678894, -0.024396324214549327)
MESH = pl.DeviceIdType.MESH
TILE = 512
ROWS = 32
COLS = 256
UNITS = 16
STRIP = 16
SBUF = 4
STAGE = 2


def horner(terms, u):
    total = jnp.full_like(u, terms[-1])
    for term in terms[-2::-1]:
        total = total * u + term
    return total


def turns_cos_sin(turns):
    part = turns - jnp.round(turns)
    square = part * part
    half_sin = part * horner(SIN_TERMS, square)
    half_cos = horner(COS_TERMS, square)
    doubled = half_sin + half_sin
    return 1.0 - doubled * half_sin, doubled * half_cos


def times(a, b):
    return a[0] * b[0] - a[1] * b[1], a[1] * b[0] + a[0] * b[1]


def twice(a):
    doubled = a[1] + a[1]
    return 1.0 - doubled * a[1], doubled * a[0]


def iteration_kernel(
    period, normalizer, step_size,
    spectra, current_in, table, blocks, offsets, slowness, weights,
    stepped_out, shrink_out,
    cs_a, cs_b, prev_cos, prev_sin, now_cos, now_sin, unit_cos, unit_sin, chain,
    tab_t, slow_8, slow_t, delay, current,
    current_b, x_all, spec_rx, sbuf, stage, own, home, gbuf, rx1, rx2, tx2, keep2, tx3, sums, shrinks,
    x_send, x_recv, y_send, y_recv, s_send, s_recv, l_stage, l_own,
    g1_send, g1_recv, g2_send, g2_recv, g3_send, g3_recv, n_send, n_recv, m_send, m_recv, l_current,
):
    me = lax.axis_index("freq")
    sta = lax.axis_index("sta")
    z, y = me // 2, me % 2
    zl, zp = z % 2, z // 2
    x, core = sta // 2, sta % 2
    tiles = cs_a.shape[1]

    def pick(ph, first, second):
        return jnp.where(ph == 0, first, second)

    def block_of(ph, fd, m):
        return pick(ph, fd // 2 * 2 + m, (fd // 4 * 2 + m) * 2 + fd % 2)

    def residue_of(ph, fd):
        return pick(ph, 2 * (fd % 2), 1 + 2 * (fd // 2 % 2))

    def member(ph):
        return pick(ph, y, zl)

    def partner(ph):
        return pick(ph, me ^ 1, me ^ 2)

    def stage_copy(ph, unit):
        slot = lax.rem(unit, STAGE)
        line = 4 * unit + residue_of(ph, partner(ph))
        return pltpu.make_async_copy(spectra.at[:, :, line, :], stage.at[ph, slot], l_stage.at[ph, slot])

    def own_copy(q, par, e):
        ph = q // 8
        line = 4 * (2 * (q % 8) + e) + residue_of(ph, me)
        return pltpu.make_async_copy(spectra.at[:, :, line, :], own.at[par, e], l_own.at[par, e])

    load = pltpu.make_async_copy(current_in, current, l_current)
    load.start()
    barrier = pltpu.get_barrier_semaphore()
    for d in range(1, 8):
        pl.semaphore_signal(barrier, inc=1, device_id=(me ^ d, sta), device_id_type=MESH)
    for d in range(1, 4):
        pl.semaphore_signal(barrier, inc=1, device_id=(me, sta ^ d), device_id_type=MESH)
    load.wait()
    for first in range(STAGE):
        for ph in range(2):
            stage_copy(ph, first).start()
    for e in range(2):
        own_copy(0, 0, e).start()
    for j in range(8):
        current_b[j // 4, j % 4] = current[j].astype(jnp.bfloat16)
    pl.semaphore_wait(barrier, 10)

    def x_remote(ph, fd, m, source, origin):
        return pltpu.make_async_remote_copy(
            current_b.at[:, residue_of(ph, fd), :, pl.ds(pl.multiple_of(16 * block_of(ph, fd, m), 16), 16), :],
            x_all.at[sta, pl.ds(8 * 2 * ph + 2 * origin, 2), :, pl.ds(16 * m, 16), :],
            x_send.at[ph, m, source], x_recv.at[ph, m, origin],
            device_id=(fd, sta), device_id_type=MESH,
        )

    def x_local(ph, m):
        return pltpu.make_async_copy(
            current_b.at[:, residue_of(ph, me), :, pl.ds(pl.multiple_of(16 * block_of(ph, me, m), 16), 16), :],
            x_all.at[sta, pl.ds(8 * 2 * ph + 2 * me, 2), :, pl.ds(16 * m, 16), :],
            x_recv.at[ph, m, me],
        )

    for ph in range(2):
        for m in range(2):
            x_local(ph, m).start()
        for d in range(1, 8):
            for m in range(2):
                x_remote(ph, me ^ d, m, d, me).start()

    def forward(ph, origin):
        for m in range(2):
            @pl.when(origin == me)
            def _():
                x_local(ph, m).wait()

            @pl.when(origin != me)
            def _():
                x_remote(ph, me, m, 1, origin).wait_recv()
        for d in range(1, 3):
            y_remote(ph, origin, d).start()

    def y_remote(ph, origin, d):
        rows = pl.ds(16 * ph + 2 * origin, 2)
        held = sta ^ 2 if d == 3 else sta
        return pltpu.make_async_remote_copy(
            x_all.at[held, rows], x_all.at[held, rows],
            y_send.at[ph, origin, d], y_recv.at[ph, origin, d],
            device_id=(me, sta ^ (2 if d == 2 else 1)), device_id_type=MESH,
        )

    def relay(q):
        ph, origin = q // 8, lax.rem(q, 8)
        y_remote(ph, origin, 2).wait_recv()
        y_remote(ph, origin, 3).start()

    def s_remote(ph, unit):
        slot = lax.rem(unit, SBUF)
        return pltpu.make_async_remote_copy(
            sbuf.at[ph, slot], spec_rx.at[ph, unit], s_send.at[ph, slot], s_recv.at[ph, unit],
            device_id=(partner(ph), sta), device_id_type=MESH,
        )

    def send_unit(ph, unit):
        stage_copy(ph, unit).wait()

        @pl.when(unit >= SBUF)
        def _():
            s_remote(ph, unit - SBUF).wait_send()

        sbuf[ph, lax.rem(unit, SBUF)] = stage[ph, lax.rem(unit, STAGE)].astype(jnp.bfloat16)
        s_remote(ph, unit).start()

        @pl.when(unit + STAGE < UNITS)
        def _():
            stage_copy(ph, unit + STAGE).start()

    tab_t[...] = jnp.transpose(jnp.bitwise_and(table[...], period - 1).astype(jnp.float32)).astype(jnp.bfloat16)
    slow_8[...] = jnp.zeros_like(slow_8)
    slow_8[0:2, :] = slowness[...]
    slow_t[...] = jnp.transpose(slow_8[...])
    cells = delay.shape[0]
    scale = 1.0 / period

    def start_chain(ph, unit, turn, cs, t, at):
        second = twice(unit)
        if ph == 0:
            third = times(unit, second)
            a = jnp.where(y == 0, third[0], unit[0]), -jnp.where(y == 0, third[1], unit[1])
            b = jnp.where(y == 0, unit[0], third[0]), jnp.where(y == 0, unit[1], third[1])
        else:
            fourth = twice(second)
            a = jnp.where(zl == 0, second[0], 1.0), jnp.where(zl == 0, -second[1], 0.0)
            b = jnp.where(zl == 0, second[0], fourth[0]), jnp.where(zl == 0, second[1], fourth[1])
        return store_pair(a, b, turn, cs, t, at, True)

    def store_pair(a, b, turn, cs, t, at, first):
        row, col, col_s = at
        one = b if first else (turn * b[0] - a[0], turn * b[1] - a[1])
        old = a if first else b
        two = turn * one[0] - old[0], turn * one[1] - old[1]
        prev_cos[t, row, col], prev_sin[t, row, col] = one
        now_cos[t, row, col], now_sin[t, row, col] = two
        for e, value in enumerate((one, two)):
            cs[e, t, row, col] = value[0].astype(jnp.bfloat16)
            cs[e, t, row, col_s] = value[1].astype(jnp.bfloat16)
        return two[0]

    def fill(cs, t, fresh):
        after = None
        for r in range(0, cells, STRIP):
            for c in range(0, TILE, 128):
                row, col, col_s = slice(r, r + STRIP), slice(c, c + 128), slice(TILE + c, TILE + c + 128)
                turn = chain[t, row, col]
                if after is not None:
                    turn = turn + after
                at = row, col, col_s
                if fresh:
                    unit = unit_cos[t, row, col], unit_sin[t, row, col]
                    if after is not None:
                        unit = unit[0] + after, unit[1]
                    last = start_chain(1, unit, turn, cs, t, at)
                else:
                    old = prev_cos[t, row, col], prev_sin[t, row, col]
                    now = now_cos[t, row, col], now_sin[t, row, col]
                    last = store_pair(old, now, turn, cs, t, at, False)
                zero = jnp.minimum(jnp.maximum(last[0:8], 0.0), 0.0)
                after = jnp.concatenate([zero] * (STRIP // 8), axis=0)

    def angles(t, _):
        lanes = pl.ds(pl.multiple_of(t * TILE, TILE), TILE)
        picks = lax.broadcasted_iota(jnp.int32, (tab_t.shape[1], TILE), 0)
        picks = jnp.where(picks == blocks[:, lanes], 1.0, 0.0).astype(jnp.bfloat16)
        delay[...] = jnp.dot(tab_t[...], picks, preferred_element_type=jnp.float32)

        def strip(index, _):
            r = pl.multiple_of(index * ROWS, ROWS)
            row = pl.ds(r, ROWS)
            slow = slow_t[row, :]
            for c in range(0, TILE, COLS):
                col, col_s = slice(c, c + COLS), slice(TILE + c, TILE + c + COLS)
                here = pl.ds(pl.multiple_of(t * TILE + c, COLS), COLS)
                geometry = offsets[0:1, here] * slow[:, 0:1] + offsets[1:2, here] * slow[:, 1:2]
                turns = delay[row, col] * scale
                unit = turns_cos_sin((delay[row, col] + geometry) * scale)
                turns = 4.0 * turns
                fourth, _ = turns_cos_sin((turns - jnp.round(turns)) + geometry * (4.0 * scale))
                turn = fourth + fourth
                unit_cos[t, row, col], unit_sin[t, row, col] = unit
                chain[t, row, col] = turn
                start_chain(0, unit, turn, cs_a, t, (row, col, col_s))
            return 0

        lax.fori_loop(0, cells // ROWS, strip, 0, unroll=4)
        send_unit(0, t)

        @pl.when(t >= 2)
        def _():
            for k in range(4):
                forward(0, 4 * (t - 2) + k)

        return 0

    lax.fori_loop(0, tiles, angles, 0)

    across = (((1,), (1,)), ((), ()))

    def g1_remote(q, par, k):
        share = 1 - core + 2 * k
        return pltpu.make_async_remote_copy(
            gbuf.at[par, share], rx1.at[lax.rem(q, 4), k], g1_send.at[par, k], g1_recv.at[lax.rem(q, 4), k],
            device_id=(me, sta ^ 1), device_id_type=MESH,
        )

    def g2_remote(q, par):
        return pltpu.make_async_remote_copy(
            tx2.at[par], rx2.at[lax.rem(q, 4)], g2_send.at[par], g2_recv.at[lax.rem(q, 4)],
            device_id=(me, sta ^ 2), device_id_type=MESH,
        )

    def g3_remote(q, m, target):
        ph = q // 8
        return pltpu.make_async_remote_copy(
            tx3.at[lax.rem(q, 8), :, :, m],
            home.at[:, residue_of(ph, me), :, pl.ds(pl.multiple_of(16 * block_of(ph, me, m), 16), 16), :],
            g3_send.at[lax.rem(q, 8), m], g3_recv.at[ph, m, me],
            device_id=(target, sta), device_id_type=MESH,
        )

    def g3_local(q, m):
        ph = q // 8
        return pltpu.make_async_copy(
            tx3.at[lax.rem(q, 8), :, :, m],
            home.at[:, residue_of(ph, me), :, pl.ds(pl.multiple_of(16 * block_of(ph, me, m), 16), 16), :],
            g3_recv.at[ph, m, me],
        )

    def g3_arrived(ph, m, origin):
        return pltpu.make_async_remote_copy(
            tx3.at[0, :, :, m],
            home.at[:, residue_of(ph, origin), :, pl.ds(pl.multiple_of(16 * block_of(ph, origin, m), 16), 16), :],
            g3_send.at[0, m], g3_recv.at[ph, m, origin],
            device_id=(me, sta), device_id_type=MESH,
        )

    def stage1(q, par):
        for k in range(2):
            g1_remote(q, par, k).start()

    def stage2(q, par):
        for k in range(2):
            g1_remote(q, par, k).wait()

        @pl.when(q >= 2)
        def _():
            g2_remote(q - 2, par).wait_send()

        slot = lax.rem(q, 4)
        tx2[par] = gbuf[par, core + 2 * (1 - x)] + rx1[slot, 1 - x]
        keep2[par] = gbuf[par, core + 2 * x] + rx1[slot, x]
        g2_remote(q, par).start()

    def stage3(q, par):
        g2_remote(q, par).wait_recv()

        @pl.when(q >= 8)
        def _():
            finish3(q - 8)

        total = (keep2[par] + rx2[lax.rem(q, 4)]) * normalizer
        target = lax.rem(q, 8)
        tx3[target] = total.reshape(tx3.shape[1:])

        @pl.when(target == me)
        def _():
            for m in range(2):
                g3_local(q, m).start()

        @pl.when(target != me)
        def _():
            for m in range(2):
                g3_remote(q, m, target).start()

    def finish3(q):
        @pl.when(lax.rem(q, 8) == me)
        def _():
            for m in range(2):
                g3_local(q, m).wait()

        @pl.when(lax.rem(q, 8) != me)
        def _():
            for m in range(2):
                g3_remote(q, m, lax.rem(q, 8)).wait_send()

    def run_pair(q, par, cs, cs_next):
        ph, p = q // 8, lax.rem(q, 8)
        mem = member(ph)

        for e in range(2):
            @pl.when(q < 15)
            def _():
                own_copy(q + 1, 1 - par, e).start()

        @pl.when(4 + 2 * q < UNITS)
        def _():
            for k in range(2):
                send_unit(0, 4 + 2 * q + k)

        @pl.when(2 * q < UNITS)
        def _():
            for k in range(2):
                send_unit(1, 2 * q + k)

        @pl.when(q < 15)
        def _():
            relay(q + 1)

        y_remote(ph, p, 1).wait_recv()
        y_remote(ph, p, 3).wait_recv()
        for e in range(2):
            s_remote(ph, 2 * p + e).wait_recv()
            own_copy(q, par, e).wait()
        gbuf[par] = jnp.zeros_like(gbuf[par])

        def body(mode, t, _):
            lanes = pl.ds(pl.multiple_of(t * TILE, TILE), TILE)
            rcats = []
            for e in range(2):
                at = 2 * q + e
                x1 = jnp.concatenate([x_all[s, at].reshape(64, 128) for s in range(4)], axis=1)
                x2 = jnp.concatenate([x1[32:], -x1[:32]], axis=0)
                acc = jnp.dot(x1, cs[e, t, :, 0:TILE], preferred_element_type=jnp.float32)
                acc += jnp.dot(x2, cs[e, t, :, TILE:], preferred_element_type=jnp.float32)
                acc = acc * normalizer
                seen = []
                for k in range(2):
                    mine = own[par, e, k, :, lanes]
                    theirs = spec_rx[ph, 2 * p + e, k, :, lanes].astype(jnp.float32)
                    seen.append(jnp.where(mem == 0, mine, theirs))
                    seen.append(jnp.where(mem == 0, theirs, mine))
                res = (acc - jnp.concatenate(seen, axis=0)).astype(jnp.bfloat16)
                rcats.append(jnp.concatenate([res, jnp.concatenate([-res[32:], res[:32]], axis=0)], axis=1))
            for e in range(2):
                back = lax.dot_general(rcats[e], cs[e, t], across, preferred_element_type=jnp.float32)
                for s in range(4):
                    gbuf[par, s, 64 * e : 64 * e + 64, :] += back[:, 128 * s : 128 * s + 128]
            if mode != "none":
                fill(cs_next, t, mode == "fresh")
            return 0

        if par == 0:
            lax.fori_loop(0, tiles, functools.partial(body, "next"), 0)
        else:
            for mode, here in (("fresh", q == 7), ("none", q == 15), ("next", (q != 7) & (q != 15))):
                @pl.when(here)
                def _():
                    lax.fori_loop(0, tiles, functools.partial(body, mode), 0)

        @pl.when(q < 8)
        def _():
            forward(1, p)

        stage1(q, par)

        @pl.when(q >= 1)
        def _():
            stage2(q - 1, 1 - par)

        @pl.when(q >= 2)
        def _():
            stage3(q - 2, par)

    def two_pairs(i, _):
        run_pair(2 * i, 0, cs_a, cs_b)
        run_pair(2 * i + 1, 1, cs_b, cs_a)
        return 0

    relay(0)
    lax.fori_loop(0, 8, two_pairs, 0)
    stage2(15, 1)
    stage3(14, 0)
    stage3(15, 1)

    for ph in range(2):
        for d in range(1, 8):
            for m in range(2):
                x_remote(ph, me ^ d, m, d, me).wait_send()
        for unit in range(UNITS - SBUF, UNITS):
            s_remote(ph, unit).wait_send()
    for ph in range(2):
        def left(origin, _):
            for d in range(1, 4):
                y_remote(ph, origin, d).wait_send()
            return 0

        lax.fori_loop(0, 8, left, 0)
    g2_remote(14, 0).wait_send()
    g2_remote(15, 1).wait_send()

    def finished(q, _):
        finish3(q)
        return 0

    lax.fori_loop(8, 16, finished, 0)
    for ph in range(2):
        for d in range(1, 8):
            for m in range(2):
                g3_arrived(ph, m, me ^ d).wait_recv()

    def step_block(w, _):
        rows = pl.ds(pl.multiple_of(w * 16, 16), 16)
        total = jnp.zeros((16, 128), jnp.float32)
        for j in range(8):
            for k in range(2):
                value = current[j, k, rows, :] - step_size * home[j // 4, j % 4, k, rows, :]
                stepped_out[j, k, rows, :] = value
                total = total + value * value
        sums[0, w] = total
        return 0

    lax.fori_loop(0, 8, step_block, 0)

    def n_remote(d):
        return pltpu.make_async_remote_copy(
            sums.at[0, me ^ d], sums.at[1, d], n_send.at[d], n_recv.at[d],
            device_id=(me ^ d, sta), device_id_type=MESH,
        )

    for d in range(1, 8):
        n_remote(d).start()
    total = sums[0, me]
    for d in range(1, 8):
        n_remote(d).wait()
        total = total + sums[1, d]
    group_norm = jnp.sqrt(total + 1e-06)
    shrinks[me] = jnp.maximum(0.0, 1.0 - step_size * weights[...] / group_norm)

    def m_remote(d, slot):
        return pltpu.make_async_remote_copy(
            shrinks.at[slot], shrinks.at[slot], m_send.at[d], m_recv.at[d],
            device_id=(me ^ d, sta), device_id_type=MESH,
        )

    for d in range(1, 8):
        m_remote(d, me).start()
    for d in range(1, 8):
        m_remote(d, me).wait_send()
        m_remote(d, me ^ d).wait_recv()
    shrink_out[...] = shrinks[...].reshape(shrink_out.shape)


def local_paired(freq_size, sta_size, spectra, current, previous, table, station_block, offsets, slowness, weights, momentum):
    period = 4 * F
    normalizer = 1.0 / math.sqrt(CELLS)
    bins, _, windows, share = current.shape
    stations = station_block.shape[0]
    cells = table.shape[1]
    step_size = CELLS / (math.sqrt(stations * sta_size) + math.sqrt(CELLS)) ** 2
    tiles = stations // TILE
    f32, bf16 = jnp.float32, jnp.bfloat16
    vm, dma = pltpu.VMEM, pltpu.SemaphoreType.DMA
    state = vm((tiles, cells, TILE), f32)
    piece = spectra.shape[1]
    inside = pl.BlockSpec(memory_space=pltpu.VMEM)
    stepped, shrink = pl.pallas_call(
        functools.partial(iteration_kernel, period, normalizer, step_size),
        out_shape=(
            jax.ShapeDtypeStruct((bins, 2, windows, share), f32),
            jax.ShapeDtypeStruct((windows, share), f32),
        ),
        in_specs=[pl.BlockSpec(memory_space=pl.ANY)] * 2 + [inside] * 5,
        out_specs=(inside, inside),
        scratch_shapes=[
            vm((2, tiles, cells, 2 * TILE), bf16),
            vm((2, tiles, cells, 2 * TILE), bf16),
            state, state, state, state, state, state, state,
            vm((cells, table.shape[0]), bf16),
            vm((8, cells), f32),
            vm((cells, 8), f32),
            vm((cells, TILE), f32),
            vm(current.shape, f32),
            vm((2, 4, 2, windows, share), bf16),
            vm((4, 32, 2, 32, share), bf16),
            vm((2, UNITS, 2, piece, stations), bf16),
            vm((2, SBUF, 2, piece, stations), bf16),
            vm((2, STAGE, 2, piece, stations), f32),
            vm((2, 2, 2, piece, stations), f32),
            vm((2, 4, 2, windows, share), f32),
            vm((2, 4, 128, share), f32),
            vm((4, 2, 128, share), f32),
            vm((4, 128, share), f32),
            vm((2, 128, share), f32),
            vm((2, 128, share), f32),
            vm((8, 2, 2, 2, 16, share), f32),
            vm((2, 8, 16, share), f32),
            vm((8, 16, share), f32),
            dma((2, 2, 8)), dma((2, 2, 8)), dma((2, 8, 4)), dma((2, 8, 4)),
            dma((2, SBUF)), dma((2, UNITS)), dma((2, STAGE)), dma((2, 2)),
            dma((2, 2)), dma((4, 2)), dma((2,)), dma((4,)), dma((8, 2)), dma((2, 2, 8)),
            dma((8,)), dma((8,)), dma((8,)), dma((8,)), dma(()),
        ],
        compiler_params=pltpu.CompilerParams(
            vmem_limit_bytes=63 * 2**20, collective_id=0, has_side_effects=True
        ),
        cost_estimate=pl.CostEstimate(
            flops=8 * 32 * 64 * cells * stations, bytes_accessed=24 * 2**20, transcendentals=0
        ),
    )(spectra, current, table, station_block.reshape(1, -1), offsets, slowness, weights.reshape(1, -1))
    estimate = stepped * shrink
    momentum_now = momentum[0]
    momentum_next = (1.0 + jnp.sqrt(1.0 + 4.0 * momentum_now * momentum_now)) / 2.0
    extrapolated = estimate + (momentum_now - 1.0) / momentum_next * (estimate - previous)
    return (estimate, extrapolated)


def solution(mesh):
    freq_size, sta_size = mesh.shape["freq"], mesh.shape["sta"]
    body = local
    if freq_size == 8 and sta_size == 4:
        body = functools.partial(local_paired, freq_size, sta_size)
    in_specs = (
        P(None, "freq", None, "sta"),
        P("freq", None, None, "sta"),
        P("freq", None, None, "sta"),
        P(),
        P("sta"),
        P(None, "sta"),
        P(),
        P("sta"),
        P(),
    )
    out_specs = (P("freq", None, None, "sta"), P("freq", None, None, "sta"))
    return jax.shard_map(body, mesh=mesh, in_specs=in_specs, out_specs=out_specs, check_vma=False)
```

```python
import functools
import math

import jax
import jax.numpy as jnp
from jax import lax
from jax.experimental import pallas as pl
from jax.experimental.pallas import tpu as pltpu
from jax.sharding import PartitionSpec as P

F = 64
CELLS = 512


def cell_block(cell_count):
    block_len = cell_count
    while block_len > 512 and block_len % 2 == 0:
        block_len = block_len // 2
    return block_len


def phases(number, delay_rows, off_rows, slow_cols, period):
    wrapped = number * delay_rows % period
    geometry = (
        off_rows[0][:, None] * slow_cols[0][None, :] + off_rows[1][:, None] * slow_cols[1][None, :]
    )
    phase_angle = (wrapped.astype(jnp.float32) + number.astype(jnp.float32) * geometry) * (
        2.0 * math.pi / period
    )
    return (jnp.cos(phase_angle).astype(jnp.bfloat16), jnp.sin(phase_angle).astype(jnp.bfloat16))


def forward_terms(cos_part, sin_part, iterate):
    window_count = iterate.shape[1]
    stacked = iterate.reshape(2 * window_count, iterate.shape[2])
    contract = (((1,), (1,)), ((), ()))
    with_cos = lax.dot_general(stacked, cos_part, contract, preferred_element_type=jnp.float32)
    with_sin = lax.dot_general(stacked, sin_part, contract, preferred_element_type=jnp.float32)
    real_part = with_cos[:window_count] + with_sin[window_count:]
    imag_part = with_cos[window_count:] - with_sin[:window_count]
    return jnp.stack([real_part, imag_part])


def adjoint_terms(cos_part, sin_part, residual):
    window_count = residual.shape[1]
    stacked = residual.reshape(2 * window_count, residual.shape[2])
    with_cos = jnp.dot(stacked, cos_part, preferred_element_type=jnp.float32)
    with_sin = jnp.dot(stacked, sin_part, preferred_element_type=jnp.float32)
    real_part = with_cos[:window_count] - with_sin[window_count:]
    imag_part = with_cos[window_count:] + with_sin[:window_count]
    return jnp.stack([real_part, imag_part])


def local(spectra, current, previous, table, station_block, offsets, slowness, weights, momentum):
    period = 4 * F
    normalizer = 1.0 / math.sqrt(CELLS)
    bin_count = current.shape[0]
    cell_share = current.shape[3]
    stations_here = station_block.shape[0]
    station_total = stations_here * lax.axis_size("sta")
    first_bin = lax.axis_index("freq") * bin_count
    relaid = lax.all_to_all(
        spectra.astype(jnp.bfloat16), "freq", split_axis=2, concat_axis=1, tiled=True
    ).astype(spectra.dtype)
    iterate_b = current.astype(jnp.bfloat16)
    segment = lax.all_gather(iterate_b, "sta", axis=3, tiled=True)
    cell_count = segment.shape[3]
    block_len = cell_block(cell_count)
    delay_rows = jnp.take(table, station_block, axis=0)
    bin_terms = []
    cos_blocks = []
    sin_blocks = []
    for add_bin_index in range(bin_count):
        cos_part, sin_part = phases(
            first_bin + add_bin_index + 1, delay_rows, offsets, slowness, period
        )
        cos_blocks.append(cos_part)
        sin_blocks.append(sin_part)
        bin_terms.append(
            forward_terms(cos_part, sin_part, segment[add_bin_index, :, :, 0:block_len])
        )
    running = jnp.stack(bin_terms)
    cos_all = jnp.stack(cos_blocks)
    sin_all = jnp.stack(sin_blocks)
    predicted, cos_all, sin_all = (running, cos_all, sin_all)
    bin_sums = []
    for bin_index in range(bin_count):
        residual = (predicted[bin_index] * normalizer - relaid[:, :, bin_index, :]).astype(
            jnp.bfloat16
        )
        bin_sums.append(
            adjoint_terms(cos_all[bin_index], sin_all[bin_index], residual) * normalizer
        )
    partial_sums = jnp.stack(bin_sums)
    summed = lax.psum(partial_sums, "sta")
    gradient = lax.dynamic_slice_in_dim(summed, lax.axis_index("sta") * cell_share, cell_share, 3)
    step_size = CELLS / (math.sqrt(station_total) + math.sqrt(CELLS)) ** 2
    stepped = current - step_size * gradient
    threshold = step_size * weights
    squares = jnp.sum(stepped * stepped, axis=(0, 1))
    group_norm = jnp.sqrt(lax.psum(squares, "freq") + 1e-06)
    estimate = stepped * jnp.maximum(0.0, 1.0 - threshold[None, :] / group_norm)
    momentum_now = momentum[0]
    momentum_next = (1.0 + jnp.sqrt(1.0 + 4.0 * momentum_now * momentum_now)) / 2.0
    extrapolated = estimate + (momentum_now - 1.0) / momentum_next * (estimate - previous)
    return (estimate, extrapolated)


SIN_TERMS = (3.1415926535362892, -5.167712764624382, 2.5501633189428987, -0.5992521977810126, 0.08205040162239277, -0.007028386120383206)
COS_TERMS = (0.9999999997799041, -4.934802137078749, 4.058709159554242, -1.335212003029471, 0.23493731372678894, -0.024396324214549327)
MESH = pl.DeviceIdType.MESH
TILE = 512
ROWS = 32
COLS = 256
UNITS = 16
STRIP = 16
SBUF = 4
STAGE = 2


def horner(terms, u):
    total = jnp.full_like(u, terms[-1])
    for term in terms[-2::-1]:
        total = total * u + term
    return total


def turns_cos_sin(turns):
    part = turns - jnp.round(turns)
    square = part * part
    half_sin = part * horner(SIN_TERMS, square)
    half_cos = horner(COS_TERMS, square)
    doubled = half_sin + half_sin
    return 1.0 - doubled * half_sin, doubled * half_cos


def times(a, b):
    return a[0] * b[0] - a[1] * b[1], a[1] * b[0] + a[0] * b[1]


def twice(a):
    doubled = a[1] + a[1]
    return 1.0 - doubled * a[1], doubled * a[0]


def iteration_kernel(
    period, normalizer, step_size,
    spectra, current_in, table, blocks, offsets, slowness, weights,
    stepped_out, shrink_out,
    cs_a, cs_b, prev_cos, prev_sin, now_cos, now_sin, unit_cos, unit_sin, chain,
    tab_t, slow_8, slow_t, delay, current,
    current_b, x_all, spec_rx, sbuf, stage, own, home, gbuf, rx1, rx2, tx2, keep2, tx3, sums, shrinks,
    x_send, x_recv, y_send, y_recv, s_send, s_recv, l_stage, l_own,
    g1_send, g1_recv, g2_send, g2_recv, g3_send, g3_recv, n_send, n_recv, m_send, m_recv, l_current,
):
    me = lax.axis_index("freq")
    sta = lax.axis_index("sta")
    z, y = me // 2, me % 2
    zl, zp = z % 2, z // 2
    x, core = sta // 2, sta % 2
    tiles = cs_a.shape[1]

    def pick(ph, first, second):
        return jnp.where(ph == 0, first, second)

    def block_of(ph, fd, m):
        return pick(ph, fd // 2 * 2 + m, (fd // 4 * 2 + m) * 2 + fd % 2)

    def residue_of(ph, fd):
        return pick(ph, 2 * (fd % 2), 1 + 2 * (fd // 2 % 2))

    def member(ph):
        return pick(ph, y, zl)

    def partner(ph):
        return pick(ph, me ^ 1, me ^ 2)

    def stage_copy(ph, unit):
        slot = lax.rem(unit, STAGE)
        line = 4 * unit + residue_of(ph, partner(ph))
        return pltpu.make_async_copy(spectra.at[:, :, line, :], stage.at[ph, slot], l_stage.at[ph, slot])

    def own_copy(q, par, e):
        ph = q // 8
        line = 4 * (2 * (q % 8) + e) + residue_of(ph, me)
        return pltpu.make_async_copy(spectra.at[:, :, line, :], own.at[par, e], l_own.at[par, e])

    load = pltpu.make_async_copy(current_in, current, l_current)
    load.start()
    barrier = pltpu.get_barrier_semaphore()
    for d in range(1, 8):
        pl.semaphore_signal(barrier, inc=1, device_id=(me ^ d, sta), device_id_type=MESH)
    for d in range(1, 4):
        pl.semaphore_signal(barrier, inc=1, device_id=(me, sta ^ d), device_id_type=MESH)
    load.wait()
    for first in range(STAGE):
        for ph in range(2):
            stage_copy(ph, first).start()
    for e in range(2):
        own_copy(0, 0, e).start()
    for j in range(8):
        current_b[j // 4, j % 4] = current[j].astype(jnp.bfloat16)
    pl.semaphore_wait(barrier, 10)

    def x_remote(ph, fd, m, source, origin):
        return pltpu.make_async_remote_copy(
            current_b.at[:, residue_of(ph, fd), :, pl.ds(pl.multiple_of(16 * block_of(ph, fd, m), 16), 16), :],
            x_all.at[sta, pl.ds(8 * 2 * ph + 2 * origin, 2), :, pl.ds(16 * m, 16), :],
            x_send.at[ph, m, source], x_recv.at[ph, m, origin],
            device_id=(fd, sta), device_id_type=MESH,
        )

    def x_local(ph, m):
        return pltpu.make_async_copy(
            current_b.at[:, residue_of(ph, me), :, pl.ds(pl.multiple_of(16 * block_of(ph, me, m), 16), 16), :],
            x_all.at[sta, pl.ds(8 * 2 * ph + 2 * me, 2), :, pl.ds(16 * m, 16), :],
            x_recv.at[ph, m, me],
        )

    for ph in range(2):
        for m in range(2):
            x_local(ph, m).start()
        for d in range(1, 8):
            for m in range(2):
                x_remote(ph, me ^ d, m, d, me).start()

    def forward(ph, origin):
        for m in range(2):
            @pl.when(origin == me)
            def _():
                x_local(ph, m).wait()

            @pl.when(origin != me)
            def _():
                x_remote(ph, me, m, 1, origin).wait_recv()
        for d in range(1, 3):
            y_remote(ph, origin, d).start()

    def y_remote(ph, origin, d):
        rows = pl.ds(16 * ph + 2 * origin, 2)
        held = sta ^ 2 if d == 3 else sta
        return pltpu.make_async_remote_copy(
            x_all.at[held, rows], x_all.at[held, rows],
            y_send.at[ph, origin, d], y_recv.at[ph, origin, d],
            device_id=(me, sta ^ (2 if d == 2 else 1)), device_id_type=MESH,
        )

    def relay(q):
        ph, origin = q // 8, lax.rem(q, 8)
        y_remote(ph, origin, 2).wait_recv()
        y_remote(ph, origin, 3).start()

    def s_remote(ph, unit):
        slot = lax.rem(unit, SBUF)
        return pltpu.make_async_remote_copy(
            sbuf.at[ph, slot], spec_rx.at[ph, unit], s_send.at[ph, slot], s_recv.at[ph, unit],
            device_id=(partner(ph), sta), device_id_type=MESH,
        )

    def send_unit(ph, unit):
        stage_copy(ph, unit).wait()

        @pl.when(unit >= SBUF)
        def _():
            s_remote(ph, unit - SBUF).wait_send()

        sbuf[ph, lax.rem(unit, SBUF)] = stage[ph, lax.rem(unit, STAGE)].astype(jnp.bfloat16)
        s_remote(ph, unit).start()

        @pl.when(unit + STAGE < UNITS)
        def _():
            stage_copy(ph, unit + STAGE).start()

    tab_t[...] = jnp.transpose(jnp.bitwise_and(table[...], period - 1).astype(jnp.float32)).astype(jnp.bfloat16)
    slow_8[...] = jnp.zeros_like(slow_8)
    slow_8[0:2, :] = slowness[...]
    slow_t[...] = jnp.transpose(slow_8[...])
    cells = delay.shape[0]
    scale = 1.0 / period

    def start_chain(ph, unit, turn, cs, t, at):
        second = twice(unit)
        if ph == 0:
            third = times(unit, second)
            a = jnp.where(y == 0, third[0], unit[0]), -jnp.where(y == 0, third[1], unit[1])
            b = jnp.where(y == 0, unit[0], third[0]), jnp.where(y == 0, unit[1], third[1])
        else:
            fourth = twice(second)
            a = jnp.where(zl == 0, second[0], 1.0), jnp.where(zl == 0, -second[1], 0.0)
            b = jnp.where(zl == 0, second[0], fourth[0]), jnp.where(zl == 0, second[1], fourth[1])
        return store_pair(a, b, turn, cs, t, at, True)

    def store_pair(a, b, turn, cs, t, at, first):
        row, col, col_s = at
        one = b if first else (turn * b[0] - a[0], turn * b[1] - a[1])
        old = a if first else b
        two = turn * one[0] - old[0], turn * one[1] - old[1]
        prev_cos[t, row, col], prev_sin[t, row, col] = one
        now_cos[t, row, col], now_sin[t, row, col] = two
        for e, value in enumerate((one, two)):
            cs[e, t, row, col] = value[0].astype(jnp.bfloat16)
            cs[e, t, row, col_s] = value[1].astype(jnp.bfloat16)
        return two[0]

    def fill(cs, t, fresh):
        after = None
        for r in range(0, cells, STRIP):
            for c in range(0, TILE, 128):
                row, col, col_s = slice(r, r + STRIP), slice(c, c + 128), slice(TILE + c, TILE + c + 128)
                turn = chain[t, row, col]
                if after is not None:
                    turn = turn + after
                at = row, col, col_s
                if fresh:
                    unit = unit_cos[t, row, col], unit_sin[t, row, col]
                    if after is not None:
                        unit = unit[0] + after, unit[1]
                    last = start_chain(1, unit, turn, cs, t, at)
                else:
                    old = prev_cos[t, row, col], prev_sin[t, row, col]
                    now = now_cos[t, row, col], now_sin[t, row, col]
                    last = store_pair(old, now, turn, cs, t, at, False)
                zero = jnp.minimum(jnp.maximum(last[0:8], 0.0), 0.0)
                after = jnp.concatenate([zero] * (STRIP // 8), axis=0)

    def angles(t, _):
        lanes = pl.ds(pl.multiple_of(t * TILE, TILE), TILE)
        picks = lax.broadcasted_iota(jnp.int32, (tab_t.shape[1], TILE), 0)
        picks = jnp.where(picks == blocks[:, lanes], 1.0, 0.0).astype(jnp.bfloat16)
        delay[...] = jnp.dot(tab_t[...], picks, preferred_element_type=jnp.float32)

        def strip(index, _):
            r = pl.multiple_of(index * ROWS, ROWS)
            row = pl.ds(r, ROWS)
            slow = slow_t[row, :]
            for c in range(0, TILE, COLS):
                col, col_s = slice(c, c + COLS), slice(TILE + c, TILE + c + COLS)
                here = pl.ds(pl.multiple_of(t * TILE + c, COLS), COLS)
                geometry = offsets[0:1, here] * slow[:, 0:1] + offsets[1:2, here] * slow[:, 1:2]
                turns = delay[row, col] * scale
                unit = turns_cos_sin((delay[row, col] + geometry) * scale)
                turns = 4.0 * turns
                fourth, _ = turns_cos_sin((turns - jnp.round(turns)) + geometry * (4.0 * scale))
                turn = fourth + fourth
                unit_cos[t, row, col], unit_sin[t, row, col] = unit
                chain[t, row, col] = turn
                start_chain(0, unit, turn, cs_a, t, (row, col, col_s))
            return 0

        lax.fori_loop(0, cells // ROWS, strip, 0, unroll=8)
        send_unit(0, t)

        @pl.when(t >= 2)
        def _():
            for k in range(4):
                forward(0, 4 * (t - 2) + k)

        return 0

    lax.fori_loop(0, tiles, angles, 0)

    across = (((1,), (1,)), ((), ()))

    def g1_remote(q, par, k):
        share = 1 - core + 2 * k
        return pltpu.make_async_remote_copy(
            gbuf.at[par, share], rx1.at[lax.rem(q, 4), k], g1_send.at[par, k], g1_recv.at[lax.rem(q, 4), k],
            device_id=(me, sta ^ 1), device_id_type=MESH,
        )

    def g2_remote(q, par):
        return pltpu.make_async_remote_copy(
            tx2.at[par], rx2.at[lax.rem(q, 4)], g2_send.at[par], g2_recv.at[lax.rem(q, 4)],
            device_id=(me, sta ^ 2), device_id_type=MESH,
        )

    def g3_remote(q, m, target):
        ph = q // 8
        return pltpu.make_async_remote_copy(
            tx3.at[lax.rem(q, 8), :, :, m],
            home.at[:, residue_of(ph, me), :, pl.ds(pl.multiple_of(16 * block_of(ph, me, m), 16), 16), :],
            g3_send.at[lax.rem(q, 8), m], g3_recv.at[ph, m, me],
            device_id=(target, sta), device_id_type=MESH,
        )

    def g3_local(q, m):
        ph = q // 8
        return pltpu.make_async_copy(
            tx3.at[lax.rem(q, 8), :, :, m],
            home.at[:, residue_of(ph, me), :, pl.ds(pl.multiple_of(16 * block_of(ph, me, m), 16), 16), :],
            g3_recv.at[ph, m, me],
        )

    def g3_arrived(ph, m, origin):
        return pltpu.make_async_remote_copy(
            tx3.at[0, :, :, m],
            home.at[:, residue_of(ph, origin), :, pl.ds(pl.multiple_of(16 * block_of(ph, origin, m), 16), 16), :],
            g3_send.at[0, m], g3_recv.at[ph, m, origin],
            device_id=(me, sta), device_id_type=MESH,
        )

    def stage1(q, par):
        for k in range(2):
            g1_remote(q, par, k).start()

    def stage2(q, par):
        for k in range(2):
            g1_remote(q, par, k).wait()

        @pl.when(q >= 2)
        def _():
            g2_remote(q - 2, par).wait_send()

        slot = lax.rem(q, 4)
        tx2[par] = gbuf[par, core + 2 * (1 - x)] + rx1[slot, 1 - x]
        keep2[par] = gbuf[par, core + 2 * x] + rx1[slot, x]
        g2_remote(q, par).start()

    def stage3(q, par):
        g2_remote(q, par).wait_recv()

        @pl.when(q >= 8)
        def _():
            finish3(q - 8)

        total = (keep2[par] + rx2[lax.rem(q, 4)]) * normalizer
        target = lax.rem(q, 8)
        tx3[target] = total.reshape(tx3.shape[1:])

        @pl.when(target == me)
        def _():
            for m in range(2):
                g3_local(q, m).start()

        @pl.when(target != me)
        def _():
            for m in range(2):
                g3_remote(q, m, target).start()

    def finish3(q):
        @pl.when(lax.rem(q, 8) == me)
        def _():
            for m in range(2):
                g3_local(q, m).wait()

        @pl.when(lax.rem(q, 8) != me)
        def _():
            for m in range(2):
                g3_remote(q, m, lax.rem(q, 8)).wait_send()

    def run_pair(q, par, cs, cs_next):
        ph, p = q // 8, lax.rem(q, 8)
        mem = member(ph)

        for e in range(2):
            @pl.when(q < 15)
            def _():
                own_copy(q + 1, 1 - par, e).start()

        @pl.when(4 + 2 * q < UNITS)
        def _():
            for k in range(2):
                send_unit(0, 4 + 2 * q + k)

        @pl.when(2 * q < UNITS)
        def _():
            for k in range(2):
                send_unit(1, 2 * q + k)

        @pl.when(q < 15)
        def _():
            relay(q + 1)

        y_remote(ph, p, 1).wait_recv()
        y_remote(ph, p, 3).wait_recv()
        for e in range(2):
            s_remote(ph, 2 * p + e).wait_recv()
            own_copy(q, par, e).wait()
        gbuf[par] = jnp.zeros_like(gbuf[par])

        def body(mode, t, _):
            lanes = pl.ds(pl.multiple_of(t * TILE, TILE), TILE)
            rcats = []
            for e in range(2):
                at = 2 * q + e
                x1 = jnp.concatenate([x_all[s, at].reshape(64, 128) for s in range(4)], axis=1)
                x2 = jnp.concatenate([x1[32:], -x1[:32]], axis=0)
                acc = jnp.dot(x1, cs[e, t, :, 0:TILE], preferred_element_type=jnp.float32)
                acc += jnp.dot(x2, cs[e, t, :, TILE:], preferred_element_type=jnp.float32)
                acc = acc * normalizer
                seen = []
                for k in range(2):
                    mine = own[par, e, k, :, lanes]
                    theirs = spec_rx[ph, 2 * p + e, k, :, lanes].astype(jnp.float32)
                    seen.append(jnp.where(mem == 0, mine, theirs))
                    seen.append(jnp.where(mem == 0, theirs, mine))
                res = (acc - jnp.concatenate(seen, axis=0)).astype(jnp.bfloat16)
                rcats.append(jnp.concatenate([res, jnp.concatenate([-res[32:], res[:32]], axis=0)], axis=1))
            for e in range(2):
                back = lax.dot_general(rcats[e], cs[e, t], across, preferred_element_type=jnp.float32)
                for s in range(4):
                    gbuf[par, s, 64 * e : 64 * e + 64, :] += back[:, 128 * s : 128 * s + 128]
            if mode != "none":
                fill(cs_next, t, mode == "fresh")
            return 0

        if par == 0:
            lax.fori_loop(0, tiles, functools.partial(body, "next"), 0)
        else:
            for mode, here in (("fresh", q == 7), ("none", q == 15), ("next", (q != 7) & (q != 15))):
                @pl.when(here)
                def _():
                    lax.fori_loop(0, tiles, functools.partial(body, mode), 0)

        @pl.when(q < 8)
        def _():
            forward(1, p)

        stage1(q, par)

        @pl.when(q >= 1)
        def _():
            stage2(q - 1, 1 - par)

        @pl.when(q >= 2)
        def _():
            stage3(q - 2, par)

    def two_pairs(i, _):
        run_pair(2 * i, 0, cs_a, cs_b)
        run_pair(2 * i + 1, 1, cs_b, cs_a)
        return 0

    relay(0)
    lax.fori_loop(0, 8, two_pairs, 0)
    stage2(15, 1)
    stage3(14, 0)
    stage3(15, 1)

    for ph in range(2):
        for d in range(1, 8):
            for m in range(2):
                x_remote(ph, me ^ d, m, d, me).wait_send()
        for unit in range(UNITS - SBUF, UNITS):
            s_remote(ph, unit).wait_send()
    for ph in range(2):
        def left(origin, _):
            for d in range(1, 4):
                y_remote(ph, origin, d).wait_send()
            return 0

        lax.fori_loop(0, 8, left, 0)
    g2_remote(14, 0).wait_send()
    g2_remote(15, 1).wait_send()

    def finished(q, _):
        finish3(q)
        return 0

    lax.fori_loop(8, 16, finished, 0)
    for ph in range(2):
        for d in range(1, 8):
            for m in range(2):
                g3_arrived(ph, m, me ^ d).wait_recv()

    def step_block(w, _):
        rows = pl.ds(pl.multiple_of(w * 16, 16), 16)
        total = jnp.zeros((16, 128), jnp.float32)
        for j in range(8):
            for k in range(2):
                value = current[j, k, rows, :] - step_size * home[j // 4, j % 4, k, rows, :]
                stepped_out[j, k, rows, :] = value
                total = total + value * value
        sums[0, w] = total
        return 0

    lax.fori_loop(0, 8, step_block, 0)

    def n_remote(d):
        return pltpu.make_async_remote_copy(
            sums.at[0, me ^ d], sums.at[1, d], n_send.at[d], n_recv.at[d],
            device_id=(me ^ d, sta), device_id_type=MESH,
        )

    for d in range(1, 8):
        n_remote(d).start()
    total = sums[0, me]
    for d in range(1, 8):
        n_remote(d).wait()
        total = total + sums[1, d]
    group_norm = jnp.sqrt(total + 1e-06)
    shrinks[me] = jnp.maximum(0.0, 1.0 - step_size * weights[...] / group_norm)

    def m_remote(d, slot):
        return pltpu.make_async_remote_copy(
            shrinks.at[slot], shrinks.at[slot], m_send.at[d], m_recv.at[d],
            device_id=(me ^ d, sta), device_id_type=MESH,
        )

    for d in range(1, 8):
        m_remote(d, me).start()
    for d in range(1, 8):
        m_remote(d, me).wait_send()
        m_remote(d, me ^ d).wait_recv()
    shrink_out[...] = shrinks[...].reshape(shrink_out.shape)


def local_paired(freq_size, sta_size, spectra, current, previous, table, station_block, offsets, slowness, weights, momentum):
    period = 4 * F
    normalizer = 1.0 / math.sqrt(CELLS)
    bins, _, windows, share = current.shape
    stations = station_block.shape[0]
    cells = table.shape[1]
    step_size = CELLS / (math.sqrt(stations * sta_size) + math.sqrt(CELLS)) ** 2
    tiles = stations // TILE
    f32, bf16 = jnp.float32, jnp.bfloat16
    vm, dma = pltpu.VMEM, pltpu.SemaphoreType.DMA
    state = vm((tiles, cells, TILE), f32)
    piece = spectra.shape[1]
    inside = pl.BlockSpec(memory_space=pltpu.VMEM)
    stepped, shrink = pl.pallas_call(
        functools.partial(iteration_kernel, period, normalizer, step_size),
        out_shape=(
            jax.ShapeDtypeStruct((bins, 2, windows, share), f32),
            jax.ShapeDtypeStruct((windows, share), f32),
        ),
        in_specs=[pl.BlockSpec(memory_space=pl.ANY)] * 2 + [inside] * 5,
        out_specs=(inside, inside),
        scratch_shapes=[
            vm((2, tiles, cells, 2 * TILE), bf16),
            vm((2, tiles, cells, 2 * TILE), bf16),
            state, state, state, state, state, state, state,
            vm((cells, table.shape[0]), bf16),
            vm((8, cells), f32),
            vm((cells, 8), f32),
            vm((cells, TILE), f32),
            vm(current.shape, f32),
            vm((2, 4, 2, windows, share), bf16),
            vm((4, 32, 2, 32, share), bf16),
            vm((2, UNITS, 2, piece, stations), bf16),
            vm((2, SBUF, 2, piece, stations), bf16),
            vm((2, STAGE, 2, piece, stations), f32),
            vm((2, 2, 2, piece, stations), f32),
            vm((2, 4, 2, windows, share), f32),
            vm((2, 4, 128, share), f32),
            vm((4, 2, 128, share), f32),
            vm((4, 128, share), f32),
            vm((2, 128, share), f32),
            vm((2, 128, share), f32),
            vm((8, 2, 2, 2, 16, share), f32),
            vm((2, 8, 16, share), f32),
            vm((8, 16, share), f32),
            dma((2, 2, 8)), dma((2, 2, 8)), dma((2, 8, 4)), dma((2, 8, 4)),
            dma((2, SBUF)), dma((2, UNITS)), dma((2, STAGE)), dma((2, 2)),
            dma((2, 2)), dma((4, 2)), dma((2,)), dma((4,)), dma((8, 2)), dma((2, 2, 8)),
            dma((8,)), dma((8,)), dma((8,)), dma((8,)), dma(()),
        ],
        compiler_params=pltpu.CompilerParams(
            vmem_limit_bytes=63 * 2**20, collective_id=0, has_side_effects=True
        ),
        cost_estimate=pl.CostEstimate(
            flops=8 * 32 * 64 * cells * stations, bytes_accessed=24 * 2**20, transcendentals=0
        ),
    )(spectra, current, table, station_block.reshape(1, -1), offsets, slowness, weights.reshape(1, -1))
    estimate = stepped * shrink
    momentum_now = momentum[0]
    momentum_next = (1.0 + jnp.sqrt(1.0 + 4.0 * momentum_now * momentum_now)) / 2.0
    extrapolated = estimate + (momentum_now - 1.0) / momentum_next * (estimate - previous)
    return (estimate, extrapolated)


def solution(mesh):
    freq_size, sta_size = mesh.shape["freq"], mesh.shape["sta"]
    body = local
    if freq_size == 8 and sta_size == 4:
        body = functools.partial(local_paired, freq_size, sta_size)
    in_specs = (
        P(None, "freq", None, "sta"),
        P("freq", None, None, "sta"),
        P("freq", None, None, "sta"),
        P(),
        P("sta"),
        P(None, "sta"),
        P(),
        P("sta"),
        P(),
    )
    out_specs = (P("freq", None, None, "sta"), P("freq", None, None, "sta"))
    return jax.shard_map(body, mesh=mesh, in_specs=in_specs, out_specs=out_specs, check_vma=False)
```
